512 devices in a mesh: seq: 16 (over y, x), exp: 32 (over z, core).
Axes of the slice: x: 4, y: 4, z: 16, core: 2. Of those that a mesh axis runs over, the one named last changes fastest.
Arguments:
- queries: bfloat16 [2048, 64, 128], P('seq', 'exp'), may hold values from -18 to 18
- cache: bfloat16 [4096, 4, 2, 128], P('seq'), may hold values from -4 to 4
- new_key_value: bfloat16 [2048, 4, 2, 128], P('seq'), may hold values from -4 to 4
- out_proj: bfloat16 [8192, 4096], P('exp', 'seq'), may hold values from -0.0625 to 0.0625
- residual: bfloat16 [2048, 4096], P('seq', 'exp'), may hold values from -3 to 3
- norm_gain: float32 [4096], replicated, may hold values from 0.1 to 1.9
- expert_ids: int32 [2048, 8], P('seq'), may hold values from 0 to 63, all different within a row; in each aligned block of 128 rows (0 to 127, 128 to 255, ...) at most 20 rows name the same one
- gates: float32 [2048, 8], P('seq'), may hold values from 0.05 to 0.5
- w_gate_up: bfloat16 [64, 4096, 1536], P('exp', 'seq'), may hold values from -0.09375 to 0.09375
- w_down: bfloat16 [64, 768, 4096], P('exp', None, 'seq'), may hold values from -0.21875 to 0.21875
Outputs:
- mixed: bfloat16 [2048, 4096], P(('seq', 'exp'))
The draws below stay inside these ranges and needn't reach their ends.
Inputs may be any that keep to these rules, and one draw needn't show every extreme that they name: `expert_ids`: within each row of 128 consecutive new tokens, at most 20 tokens name one expert, a bound that some row reaches; each token names 8 different experts.
All inputs are finite; a program needn't handle non-finite values.
Results may differ from the reference program's by a relative error of at most 0.039.
Values may be sent and summed in bfloat16 or wider, within the bound.
No kernel may reach another device: no remote copies, remote signals or barrier semaphores. Data moves between devices by JAX's collectives and lax.ppermute only.
A program may use at most 64 MiB of HBM per device.

```python
import math
import jax
import jax.numpy as jnp
import numpy as np
from jax import lax

D = 4096
QUERY_HEADS = 64
KEY_VALUE_HEADS = 4
HEAD_SIZE = 128
FF = 768
TOP = 8
EXP_DEV = 2
Q_DEV = 128
EXPERTS = 64
HQ_DEV = 2
NEW_TOKENS = 2048
CACHED_TOKENS = 4096
CAP = 20
N_SEQ = 16
N_EXP = 32


def draw_queries(key, part):
    key = jax.random.fold_in(key, 11)
    value_rows = 2.5 * jax.random.truncated_normal(key, -4.0, 4.0, (NEW_TOKENS, QUERY_HEADS, HEAD_SIZE), jnp.float32)
    return value_rows.astype(jnp.bfloat16)


def draw_cache(key, part):
    key = jax.random.fold_in(key, 12)
    value_rows = jax.random.truncated_normal(key, -4.0, 4.0, (CACHED_TOKENS, KEY_VALUE_HEADS, 2, HEAD_SIZE), jnp.float32)
    return value_rows.astype(jnp.bfloat16)


def block_levels(stream_key, dims, shards, least, high):
    def one(dim, blocks):
        draws = jax.random.uniform(jax.random.fold_in(jax.random.fold_in(stream_key, 6), dim), (blocks,), jnp.float32, least / len(shards), high / len(shards))
        return jnp.repeat(jnp.exp(draws), dims[dim] // blocks).reshape((-1,) + (1,) * (len(dims) - dim - 1))

    gain = one(*shards[0])
    for cut in shards[1:]:
        gain = gain * one(*cut)
    return gain


def routed_block(stream_key, own, number, rows, amount, top, bound, slope):
    ranking = jax.random.permutation(stream_key, amount)
    heavy_load, ordinary = shares(amount, rows * top, bound, slope, True), shares(amount, rows * top, bound, slope, False)
    places = jnp.arange(amount)

    def named(lengths, turn):
        used = int((lengths > 0).sum())
        fixed = max(1, used // 4)
        shifted = fixed + (places - fixed + turn * (used - fixed)) % max(1, amount - fixed)
        return jnp.zeros((amount,), jnp.int32).at[ranking[jnp.where(places < fixed, places, shifted)]].set(jnp.asarray(lengths, jnp.int32))

    lengths = jnp.where(number % 4 == 0, named(heavy_load, number // 4), named(ordinary, number - number // 4 - 1))
    mixed = jax.random.permutation(jax.random.fold_in(own, 3), amount)
    source_of, receiver = mixed[0:amount // 2 * 2:2], mixed[1:amount // 2 * 2:2]
    room = jnp.minimum(lengths[source_of] - 1, bound - lengths[receiver]) // 2
    room = jnp.where((source_of == ranking[0]) | (receiver == ranking[0]) | (lengths[receiver] == 0), 0, jnp.maximum(room, 0))
    shifted = jax.random.randint(jax.random.fold_in(own, 4), (amount // 2,), 0, 1 << 20) % (room + 1)
    lengths = lengths.at[source_of].add(-shifted).at[receiver].add(shifted)
    items = jnp.searchsorted(jnp.cumsum(lengths), jnp.arange(rows * top), side="right").astype(jnp.int32)
    grid = items.reshape(top, rows).T
    grid = grid[jax.random.permutation(jax.random.fold_in(own, 1), rows)]
    turn = jax.random.randint(jax.random.fold_in(own, 2), (rows, 1), 0, top)
    return jnp.take_along_axis(grid, (jnp.arange(top)[None, :] + turn) % top, axis=1)


def shares(count, total, most, slope, full):
    loads = [(1 << 20) // math.isqrt(rank ** slope) + 1 for rank in range(1, count + 1)]
    largest = most if full else min(most, max(-(-total // count), total * loads[0] // sum(loads)))
    least = 1 if total - largest >= count - 1 else 0
    counts, rest = [largest] + [least] * (count - 1), total - largest - least * (count - 1)
    while rest > 0:
        candidates = [i for i in range(1, count) if counts[i] < largest] or [i for i in range(1, count) if counts[i] < most]
        whole, budget = sum([loads[i] for i in candidates]), rest
        for i in candidates:
            addition = min(most - counts[i], max(1, budget * loads[i] // whole), rest)
            counts[i] = counts[i] + addition
            rest = rest - addition
    return np.array(counts)


def bell_draw(rng, shape, scale, reach, pieces=(), kind=jnp.bfloat16):
    drawn = scale * jax.random.normal(rng, shape, jnp.float32)
    if pieces:
        drawn = drawn * block_levels(rng, shape, pieces, -0.22, 0.18)
    return jnp.clip(drawn, -reach, reach).astype(kind)


def setup_inputs(seed: int = 0) -> dict:
    key_list = jax.random.split(jax.random.key(seed), 11)
    queries = draw_queries(jax.random.fold_in(key_list[10], 71), 0)
    cache = draw_cache(jax.random.fold_in(key_list[10], 71), 0)
    new_key_value = bell_draw(key_list[2], (NEW_TOKENS, KEY_VALUE_HEADS, 2, HEAD_SIZE), 1.0, 4.0, ((0, 16),))
    out_proj = bell_draw(key_list[3], (QUERY_HEADS * HEAD_SIZE, D), (QUERY_HEADS * HEAD_SIZE) ** -0.5, 0.0625, ((0, 32), (1, 16)))
    residual = bell_draw(key_list[4], (NEW_TOKENS, D), 0.5, 3.0, ((0, 16), (1, 32)))
    norm_gain = jnp.clip(1.0 + 0.18 * jax.random.normal(key_list[5], (D,), jnp.float32), 0.1, 1.9)
    expert_ids_keys = jax.random.split(jax.random.fold_in(key_list[6], 1), NEW_TOKENS // Q_DEV)
    expert_ids_turns = jax.random.permutation(jax.random.fold_in(key_list[6], 3), NEW_TOKENS // Q_DEV)
    expert_ids = jax.vmap(lambda own, number: routed_block(jax.random.fold_in(key_list[6], 2), own, number, Q_DEV, EXPERTS, TOP, CAP, 1))(expert_ids_keys, expert_ids_turns).reshape((NEW_TOKENS, TOP))
    gates = jnp.clip(jnp.exp(math.log(0.5) - 2.3025851 * jax.random.uniform(key_list[7], (NEW_TOKENS, TOP), jnp.float32) ** block_levels(key_list[7], (NEW_TOKENS, TOP), ((0, 16),), -0.2, 0.2)), 0.05, 0.5)
    w_gate_up = bell_draw(key_list[8], (EXPERTS, D, 2 * FF), D ** -0.5, 0.09375, ((0, 32), (1, 16)))
    w_down = bell_draw(key_list[9], (EXPERTS, FF, D), FF ** -0.5, 0.21875, ((0, 32), (2, 16)))
    return dict(queries=queries, cache=cache, new_key_value=new_key_value, out_proj=out_proj, residual=residual, norm_gain=norm_gain, expert_ids=expert_ids, gates=gates, w_gate_up=w_gate_up, w_down=w_down)


def reference(queries, cache, new_key_value, out_proj, residual, norm_gain, expert_ids, gates, w_gate_up, w_down):
    scale_factor = 1.0 / math.sqrt(HEAD_SIZE)
    group_width = QUERY_HEADS // KEY_VALUE_HEADS
    key_rows = jnp.concatenate([cache, new_key_value], axis=0)
    key_pos = jnp.concatenate([jnp.full((CACHED_TOKENS,), -1, jnp.int32), jnp.arange(NEW_TOKENS, dtype=jnp.int32)])
    query_pos = jnp.arange(NEW_TOKENS, dtype=jnp.int32)
    visible = key_pos[None, :] <= query_pos[:, None]

    def one_head(head_index):
        kv_index = head_index // group_width
        head_queries = lax.dynamic_index_in_dim(queries, head_index, 1, keepdims=False)
        head_keys = lax.dynamic_index_in_dim(key_rows, kv_index, 1, keepdims=False)
        scores = jnp.dot(head_queries, head_keys[:, 0].T, preferred_element_type=jnp.float32) * scale_factor
        scores = jnp.where(visible, scores, -jnp.inf)
        highest = lax.optimization_barrier(jnp.max(scores, axis=1, keepdims=True))
        probs = jnp.where(visible, jnp.exp(scores - highest), 0.0)
        denominator = lax.optimization_barrier(jnp.sum(probs, axis=1, keepdims=True))
        weighted = jnp.dot(probs.astype(jnp.bfloat16), head_keys[:, 1], preferred_element_type=jnp.float32)
        return (weighted / denominator).astype(jnp.bfloat16)
    attended = lax.map(one_head, jnp.arange(QUERY_HEADS, dtype=jnp.int32))
    grouped = attended.reshape(N_EXP, HQ_DEV, NEW_TOKENS, HEAD_SIZE)
    projection = out_proj.reshape(N_EXP, HQ_DEV * HEAD_SIZE, D)

    def add_group(running, group_index):
        block_rows = jnp.transpose(grouped[group_index], (1, 0, 2)).reshape(NEW_TOKENS, HQ_DEV * HEAD_SIZE)
        head_part = jnp.dot(block_rows, projection[group_index], preferred_element_type=jnp.float32).astype(jnp.bfloat16)
        head_part = lax.optimization_barrier(head_part)
        return (running + head_part.astype(jnp.float32), None)
    head_sum, _ = lax.scan(add_group, jnp.zeros((NEW_TOKENS, D), jnp.float32), jnp.arange(N_EXP, dtype=jnp.int32))
    hidden_state = (residual.astype(jnp.float32) + head_sum).astype(jnp.bfloat16)
    state_f = hidden_state.astype(jnp.float32)
    mean_square = lax.optimization_barrier(jnp.mean(state_f * state_f, axis=1, keepdims=True))
    normed = (state_f * lax.rsqrt(mean_square + 1e-06) * norm_gain).astype(jnp.bfloat16)
    token_rows = normed.reshape(N_SEQ, Q_DEV, D).astype(jnp.float32)
    id_rows = expert_ids.reshape(N_SEQ, Q_DEV, TOP)
    gate_rows = gates.reshape(N_SEQ, Q_DEV, TOP)
    slot_range = jnp.arange(CAP, dtype=jnp.int32)
    slice_width = D // N_SEQ

    def one_expert(expert):
        chosen = id_rows == expert
        taken = lax.optimization_barrier(jnp.sum(chosen.astype(jnp.int32), axis=2))
        weight = lax.optimization_barrier(jnp.sum(jnp.where(chosen, gate_rows, 0.0), axis=2))
        slot = jnp.cumsum(taken, axis=1) - taken
        select = ((slot[:, None, :] == slot_range[None, :, None]) & (taken[:, None, :] > 0)).astype(jnp.float32)
        dispatched = jnp.einsum('rcq,rqd->rcd', select, token_rows).astype(jnp.bfloat16)
        block_list = dispatched.reshape(N_SEQ * CAP, N_SEQ, slice_width).astype(jnp.float32)
        weight_block_list = w_gate_up[expert].reshape(N_SEQ, slice_width, 2 * FF).astype(jnp.float32)
        partial_list = jnp.einsum('sym,ymu->ysu', block_list, weight_block_list).astype(jnp.bfloat16)
        partial_list = lax.optimization_barrier(partial_list)
        gate_up = lax.optimization_barrier(jnp.sum(partial_list.astype(jnp.float32), axis=0))
        activation = (jax.nn.silu(gate_up[:, :FF]) * gate_up[:, FF:]).astype(jnp.bfloat16)
        expert_out = jnp.dot(activation, w_down[expert], preferred_element_type=jnp.float32).astype(jnp.bfloat16)
        returned = expert_out.reshape(N_SEQ, CAP, D).astype(jnp.float32)
        weighted_select = select * weight[:, None, :]
        return jnp.einsum('rcq,rcd->rqd', weighted_select, returned).reshape(NEW_TOKENS, D)

    def add_experts(running, group_index):
        expert_part = jnp.zeros((NEW_TOKENS, D), jnp.float32)
        for member in range(EXP_DEV):
            expert_part = expert_part + one_expert(group_index * EXP_DEV + member)
        rounded = lax.optimization_barrier(expert_part.astype(jnp.bfloat16))
        return (running + rounded.astype(jnp.float32), None)
    expert_sum, _ = lax.scan(add_experts, jnp.zeros((NEW_TOKENS, D), jnp.float32), jnp.arange(N_EXP, dtype=jnp.int32))
    return (hidden_state.astype(jnp.float32) + expert_sum).astype(jnp.bfloat16)
```

```python
import functools
import math

import jax
import jax.numpy as jnp
from jax import lax
from jax.experimental import pallas as pl
from jax.experimental.pallas import tpu as pltpu
from jax.sharding import PartitionSpec as P

QUERY_HEADS = 64
KEY_VALUE_HEADS = 4
FLOOR = -1e30
VMEM_BYTES = 56 * 1024 * 1024
f32 = jnp.float32
bf16 = jnp.bfloat16


def run(body, out_shape, *operands, place=None, flops=0, moved=0, scratch=(), name=None):
    vmem = pl.BlockSpec(memory_space=pltpu.VMEM)
    smem = pl.BlockSpec(memory_space=pltpu.SMEM)
    placed = [] if place is None else [place]
    return pl.pallas_call(
        body,
        out_shape=out_shape,
        in_specs=[smem] * len(placed) + [vmem] * len(operands),
        out_specs=jax.tree.map(lambda _: vmem, out_shape),
        scratch_shapes=list(scratch),
        compiler_params=pltpu.CompilerParams(vmem_limit_bytes=VMEM_BYTES),
        cost_estimate=pl.CostEstimate(flops=flops, bytes_accessed=moved, transcendentals=0),
        name=name,
    )(*placed, *operands)


def shape(dims, dtype=bf16):
    return jax.ShapeDtypeStruct(dims, dtype)


def attend_half(place_ref, q_ref, kv_ref, *refs, first, rows, cached, fresh, scale):
    if first:
        top_ref, sum_ref, acc_ref, s_ref = refs
    else:
        top_in, sum_in, acc_in, extra_ref, out_ref, s_ref = refs
    shards, _, span, width = kv_ref.shape
    heads = q_ref.shape[0]
    seq_index, half = place_ref[0], place_ref[1]
    total = heads * rows
    q = q_ref[...].reshape(total, width)
    per = 4
    wide = per * span
    lane = lax.broadcasted_iota(jnp.int32, (1, wide), 1)
    query_pos = seq_index * rows + lax.broadcasted_iota(jnp.int32, (total, 1), 0) % rows
    top = jnp.full((total, 128), FLOOR, f32)
    for part in range(shards // per):
        keys = kv_ref[part * per : (part + 1) * per, 0].reshape(wide, width)
        s = lax.dot_general(q, keys, (((1,), (1,)), ((), ())), preferred_element_type=f32)
        within = lane % span
        pos = (part * per + lane // span) * rows + half * fresh + within - cached
        pos = jnp.where(within < cached, -1, pos)
        s = jnp.where(pos <= query_pos, s, FLOOR)
        s_ref[:, part * wide : (part + 1) * wide] = s
        for k in range(wide // 128):
            top = jnp.maximum(top, s[:, k * 128 : (k + 1) * 128])
    top = jnp.max(top, axis=1, keepdims=True)
    factor = scale * math.log2(math.e)
    if first:
        new_top = top
    else:
        old_top = top_in[:, 0:1]
        new_top = jnp.maximum(top, old_top)
    acc = jnp.zeros((total, width), f32)
    sums = jnp.zeros((total, 128), f32)
    for part in range(shards // per):
        values = kv_ref[part * per : (part + 1) * per, 1].reshape(wide, width)
        p = jnp.exp2((s_ref[:, part * wide : (part + 1) * wide] - new_top) * factor)
        for k in range(wide // 128):
            sums = sums + p[:, k * 128 : (k + 1) * 128]
        acc = acc + jnp.dot(p.astype(bf16), values, preferred_element_type=f32)
    row_sum = jnp.sum(sums, axis=1, keepdims=True)
    if first:
        top_ref[...] = jnp.broadcast_to(new_top, (total, 128))
        sum_ref[...] = jnp.broadcast_to(row_sum, (total, 128))
        acc_ref[...] = acc
    else:
        shrink = jnp.exp2((old_top - new_top) * factor)
        row_sum = row_sum + sum_in[:, 0:1] * shrink
        acc = acc + acc_in[...] * shrink
        attended = (acc / row_sum).astype(bf16)
        extra = extra_ref[...]
        for k in range(out_ref.shape[0]):
            for h in range(heads):
                out_ref[k, 0:rows, h * width : (h + 1) * width] = attended[h * rows : (h + 1) * rows]
            out_ref[k, rows:, :] = extra


def project(place_ref, got_ref, w_ref, keep_ref, send_ref, table_ref, *, rows):
    shards = got_ref.shape[0]
    half = place_ref[1]
    w = w_ref[...]
    width = w.shape[1] // 2
    group = 4
    for g in range(shards // group):
        x = got_ref[g * group : (g + 1) * group, 0:rows, :].reshape(group * rows, w.shape[0])
        y = jnp.dot(x, w, preferred_element_type=f32)
        low, high = y[:, :width], y[:, width:]
        keep = jnp.where(half == 0, low, high).astype(bf16)
        send = jnp.where(half == 0, high, low).astype(bf16)
        keep_ref[g * group : (g + 1) * group] = keep.reshape(group, rows, width)
        send_ref[g * group : (g + 1) * group] = send.reshape(group, rows, width)
    for j in range(shards // 2):
        table_ref[j] = got_ref[2 * j, rows:, :].astype(f32) + got_ref[2 * j + 1, rows:, :].astype(f32)


def add_state(got_ref, residual_ref, out_ref):
    total = residual_ref[...].astype(f32)
    for k in range(got_ref.shape[0]):
        total = total + got_ref[k].astype(f32)
    out_ref[...] = total.astype(bf16)


def dispatch(place_ref, own_ref, other_ref, ids_ref, state_ref, out_ref, *, capacity):
    half = place_ref[1]
    own, other = own_ref[...], other_ref[...]
    low = jnp.where(half == 0, own.astype(f32), other.astype(f32)).astype(bf16)
    high = jnp.where(half == 0, other.astype(f32), own.astype(f32)).astype(bf16)
    state = jnp.concatenate([low, high], axis=1)
    state_ref[...] = state
    tokens = own.shape[0]
    chips = out_ref.shape[0] // (2 * capacity)
    ids = ids_ref[...].astype(f32).astype(jnp.int32)
    before = (
        lax.broadcasted_iota(jnp.int32, (tokens, tokens), 0)
        < lax.broadcasted_iota(jnp.int32, (tokens, tokens), 1)
    ).astype(f32).astype(bf16)
    codes = []
    for member in range(2):
        expert = lax.broadcasted_iota(jnp.int32, (chips, tokens), 0) * 4 + 2 * half + member
        taken = jnp.zeros((chips, tokens), f32)
        for k in range(ids.shape[0]):
            taken = taken + (expert == ids[k : k + 1, :]).astype(f32)
        slot = jnp.dot(taken.astype(bf16), before, preferred_element_type=f32)
        codes.append(jnp.where(taken > 0, slot.astype(jnp.int32) + member * capacity, -1))
    slots = lax.broadcasted_iota(jnp.int32, (chips, 2 * capacity, tokens), 1)
    chosen = (codes[0][:, None, :] == slots) | (codes[1][:, None, :] == slots)
    select = chosen.astype(f32).reshape(chips * 2 * capacity, tokens).astype(bf16)
    out_ref[...] = jnp.dot(select, state, preferred_element_type=f32).astype(bf16)


def gate_up(x_ref, gain_ref, w_ref, out_ref, *, capacity):
    slots = x_ref.shape[0]
    columns = w_ref.shape[2]
    x = x_ref[...].astype(f32)
    squares = jnp.sum(x * x, axis=1, keepdims=True)
    scaled = (x * gain_ref[...]).astype(bf16)
    second = lax.broadcasted_iota(jnp.int32, (slots, 1), 0) % (2 * capacity) >= capacity
    step = 256
    for k in range(columns // step):
        cut = slice(k * step, (k + 1) * step)
        a = jnp.dot(scaled, w_ref[0, :, cut], preferred_element_type=f32)
        b = jnp.dot(scaled, w_ref[1, :, cut], preferred_element_type=f32)
        out_ref[:, cut] = jnp.where(second, b, a).astype(bf16)
    high = squares.astype(bf16).astype(f32)
    lane = lax.broadcasted_iota(jnp.int32, (slots, 128), 1)
    out_ref[:, columns:] = jnp.where(lane < 64, high, squares - high).astype(bf16)


def activate(got_ref, out_ref, *, features):
    blocks, slots, columns = got_ref.shape
    hidden = (columns - 128) // 2

    def total(start, size):
        value = got_ref[0, :, start : start + size].astype(f32)
        for k in range(1, blocks):
            value = value + got_ref[k, :, start : start + size].astype(f32)
        return value

    pieces = total(2 * hidden, 128)
    squares = pieces[:, 0:1] + pieces[:, 64:65]
    norm = lax.rsqrt(squares / features + 1e-6)
    for start in range(0, hidden, 128):
        gate = total(start, 128) * norm
        up = total(hidden + start, 128) * norm
        value = (gate / (1.0 + jnp.exp(-gate)) * up).astype(bf16)
        for k in range(out_ref.shape[0]):
            out_ref[k, :, start : start + 128] = value


def combine(place_ref, x_ref, w_ref, table_ref, state_ref, keep_ref, send_ref, *, capacity):
    half, chip = place_ref[1], place_ref[2]
    pairs = table_ref.shape[0]
    slots = 2 * 2 * capacity
    tokens = state_ref.shape[0]
    width = w_ref.shape[2]
    chips = keep_ref.shape[0]
    size = 2 * tokens
    x = x_ref[...]
    second = lax.broadcasted_iota(jnp.int32, (x.shape[0], 1), 0) % (2 * capacity) >= capacity
    y = jnp.where(
        second,
        jnp.dot(x, w_ref[1], preferred_element_type=f32),
        jnp.dot(x, w_ref[0], preferred_element_type=f32),
    )
    place = lax.broadcasted_iota(jnp.int32, (size, tokens), 0)
    token = (place % tokens // 8) * 8 + place // tokens * 4 + place % 4
    mine = ((place % 8 // 4) == chip % 2) & (place // tokens == half)
    column = lax.broadcasted_iota(jnp.int32, (size, tokens), 1)
    own = jnp.dot(
        ((token == column) & mine).astype(f32).astype(bf16), state_ref[...], preferred_element_type=f32
    )
    slot = lax.broadcasted_iota(jnp.int32, (slots, size), 0) + 1
    for j in range(pairs):
        table = table_ref[j]
        code = table.astype(jnp.int32)
        hit_a = slot == code[0:1, :]
        hit_b = slot == code[1:2, :]
        weight_a = table[2:3, :] + table[3:4, :] + table[4:5, :]
        weight_b = table[5:6, :] + table[6:7, :] + table[7:8, :]
        weight = jnp.where(hit_a, weight_a, 0.0) + jnp.where(hit_b, weight_b, 0.0)
        weight = jnp.sum(weight, axis=1, keepdims=True)
        rows = (y[j * slots : (j + 1) * slots] * weight).astype(bf16)
        select = (hit_a | hit_b).astype(f32).astype(bf16)
        part = lax.dot_general(select, rows, (((0,), (0,)), ((), ())), preferred_element_type=f32)
        part = part + jnp.where(j == chip // 2, own, 0.0)
        low, high = part[:tokens], part[tokens:]
        keep = jnp.where(half == 0, low, high).astype(bf16)
        send = jnp.where(half == 0, high, low).astype(bf16)
        keep_ref[:, j * 8 : (j + 1) * 8, :] = keep.reshape(chips, 8, width)
        send_ref[:, j * 8 : (j + 1) * 8, :] = send.reshape(chips, 8, width)


def local(
    queries,
    cache,
    new_key_value,
    out_proj,
    residual,
    norm_gain,
    expert_ids,
    gates,
    w_gate_up,
    w_down,
):
    n_seq, n_exp = lax.axis_size("seq"), lax.axis_size("exp")
    n_chip = n_exp // 2
    seq_index, exp_index = lax.axis_index("seq"), lax.axis_index("exp")
    core, chip = exp_index % 2, exp_index // 2
    place = jnp.stack([seq_index, core, chip]).astype(jnp.int32)
    other_place = jnp.stack([seq_index, 1 - core, chip]).astype(jnp.int32)
    rows, heads, width = queries.shape
    top_k = expert_ids.shape[1]
    features = norm_gain.shape[0]
    members, feature_block, gate_columns = w_gate_up.shape
    hidden_units = w_down.shape[1]
    capacity = 5 * rows * top_k // (4 * members * n_exp)
    swap = [(i, i ^ 1) for i in range(n_exp)]
    chips = [[2 * z + c for z in range(n_chip)] for c in range(2)]
    turn = [
        (s * n_exp + e, (e // 2) * n_exp + 2 * s + e % 2) for s in range(n_seq) for e in range(n_exp)
    ]

    def over_chips(value):
        return lax.all_to_all(value, "exp", 0, 0, tiled=True, axis_index_groups=chips)

    def over_seq(value):
        return lax.all_to_all(value, "seq", 0, 0, tiled=True)

    with jax.named_scope("turn_residual"):
        packed = jnp.concatenate([residual, expert_ids.T.astype(bf16)], axis=0)
        turned = lax.ppermute(packed, ("seq", "exp"), turn)

    with jax.named_scope("key_values"):
        group = exp_index * heads // (QUERY_HEADS // KEY_VALUE_HEADS)
        cached, fresh = cache.shape[0] // 2, rows // 2
        own_cache = lax.dynamic_slice(
            cache, (core * cached, group, 0, 0), (cached, 1, 2, width)
        ).reshape(cached, 2, width)
        own_fresh = lax.dynamic_slice(
            new_key_value, (core * fresh, group, 0, 0), (fresh, 1, 2, width)
        ).reshape(fresh, 2, width)
        own_kv = jnp.concatenate([own_cache, own_fresh], axis=0).transpose(1, 0, 2)
        half_kv = over_seq(jnp.broadcast_to(own_kv[None], (n_seq,) + own_kv.shape))
        other_kv = lax.ppermute(half_kv, "exp", swap)

    with jax.named_scope("tables"):
        lines = []
        weights = []
        for member in range(2):
            chosen = expert_ids == exp_index * 2 + member
            taken = jnp.sum(chosen.astype(jnp.int32), axis=1)
            slot = jnp.cumsum(taken) - taken
            code = slot + member * capacity + (seq_index % 2) * 2 * capacity + 1
            lines.append(jnp.where(taken > 0, code, 0).astype(f32))
            weight = jnp.sum(jnp.where(chosen, gates, 0.0), axis=1)
            first = lax.reduce_precision(weight, 8, 7)
            second = lax.reduce_precision(weight - first, 8, 7)
            weights += [first, second, weight - first - second]
        table = jnp.stack(lines + weights).reshape(8, n_chip, 2, 1, 4).transpose(0, 2, 1, 3, 4)
        spot = (jnp.arange(2) == seq_index % 2).astype(f32).reshape(1, 1, 1, 2, 1)
        extra = (table * spot).reshape(8, 2 * rows).astype(bf16)

    with jax.named_scope("attention"):
        q = queries.transpose(1, 0, 2)
        total = rows * heads
        span = cached + fresh
        half_attend = functools.partial(
            attend_half, rows=rows, cached=cached, fresh=fresh, scale=1.0 / math.sqrt(width)
        )
        flops = 4 * total * n_seq * span * width
        scores = pltpu.VMEM((total, n_seq * span), f32)
        state = run(
            functools.partial(half_attend, first=True),
            [shape((total, 128), f32), shape((total, 128), f32), shape((total, width), f32)],
            q,
            half_kv,
            place=place,
            flops=flops,
            moved=half_kv.size * 2,
            scratch=[scores],
            name="attend_first",
        )
        attended = run(
            functools.partial(half_attend, first=False),
            shape((n_seq, rows + 8, heads * width)),
            q,
            other_kv,
            *state,
            extra,
            place=other_place,
            flops=flops,
            moved=half_kv.size * 2,
            scratch=[scores],
            name="attend_second",
        )

    with jax.named_scope("projection"):
        got = over_seq(attended)
        columns = shape((n_seq, rows, feature_block // 2))
        keep, send, tables = run(
            functools.partial(project, rows=rows),
            [columns, columns, shape((n_seq // 2, 8, 2 * rows), f32)],
            got,
            out_proj,
            place=place,
            name="project",
        )
        paired = (keep.astype(f32) + lax.ppermute(send, "exp", swap).astype(f32)).astype(bf16)
        own_state = run(
            add_state,
            shape((rows, feature_block // 2)),
            over_chips(paired),
            turned[:rows],
            name="add_state",
        )
        other_state = lax.ppermute(own_state, "exp", swap)

    with jax.named_scope("gate_up"):
        slots = 2 * capacity
        state, outgoing = run(
            functools.partial(dispatch, capacity=capacity),
            [shape((rows, feature_block)), shape((n_chip * slots, feature_block))],
            own_state,
            other_state,
            turned[rows:],
            place=place,
            name="dispatch",
        )
        incoming = over_chips(outgoing.reshape(n_chip, slots, feature_block))
        gain = lax.dynamic_slice(norm_gain, (seq_index * feature_block,), (feature_block,))
        partial = run(
            functools.partial(gate_up, capacity=capacity),
            shape((n_seq * slots, gate_columns + 128)),
            incoming.reshape(n_seq * slots, feature_block),
            gain.reshape(1, -1),
            w_gate_up,
            name="gate_up",
        )
        sums = over_seq(partial.reshape(n_seq, slots, gate_columns + 128))

    with jax.named_scope("down"):
        active = run(
            functools.partial(activate, features=features),
            shape((n_seq, slots, hidden_units)),
            sums,
            name="activate",
        )
        line = shape((n_chip, n_seq * 4, feature_block))
        keep, send = run(
            functools.partial(combine, capacity=capacity),
            [line, line],
            over_seq(active).reshape(n_seq * slots, hidden_units),
            w_down,
            tables,
            state,
            place=place,
            name="combine",
        )

    with jax.named_scope("output"):
        paired = (keep.astype(f32) + lax.ppermute(send, "exp", swap).astype(f32)).astype(bf16)
        mixed = jnp.sum(over_chips(paired).astype(f32), axis=0).astype(bf16)
        mixed = over_seq(mixed.reshape(n_seq, 4, feature_block))
        return mixed.transpose(1, 0, 2).reshape(4, features)


def solution(mesh):
    in_specs = (
        P("seq", "exp", None),
        P("seq", None, None, None),
        P("seq", None, None, None),
        P("exp", "seq"),
        P("seq", "exp"),
        P(),
        P("seq", None),
        P("seq", None),
        P("exp", "seq", None),
        P("exp", None, "seq"),
    )
    out_specs = P(("seq", "exp"), None)
    return jax.shard_map(local, mesh=mesh, in_specs=in_specs, out_specs=out_specs, check_vma=False)
```

```python
import functools
import math

import jax
import jax.numpy as jnp
import numpy as np
from jax import lax
from jax.experimental import pallas as pl
from jax.experimental.pallas import tpu as pltpu
from jax.sharding import PartitionSpec as P

QUERY_HEADS = 64
KEY_VALUE_HEADS = 4
FLOOR = -1e30
VMEM_BYTES = 56 * 1024 * 1024
f32 = jnp.float32
bf16 = jnp.bfloat16


def run(body, out_shape, *operands, place=None, flops=0, moved=0, scratch=(), name=None):
    vmem = pl.BlockSpec(memory_space=pltpu.VMEM)
    smem = pl.BlockSpec(memory_space=pltpu.SMEM)
    placed = [] if place is None else [place]
    return pl.pallas_call(
        body,
        out_shape=out_shape,
        in_specs=[smem] * len(placed) + [vmem] * len(operands),
        out_specs=jax.tree.map(lambda _: vmem, out_shape),
        scratch_shapes=list(scratch),
        compiler_params=pltpu.CompilerParams(vmem_limit_bytes=VMEM_BYTES),
        cost_estimate=pl.CostEstimate(flops=flops, bytes_accessed=moved, transcendentals=0),
        name=name,
    )(*placed, *operands)


def shape(dims, dtype=bf16):
    return jax.ShapeDtypeStruct(dims, dtype)


def attend(place_ref, q_ref, kv_ref, out_ref, s_ref, *, rows, cached, scale):
    sides, _, span, width = kv_ref.shape
    blocks = q_ref.shape[0]
    seq_index = place_ref[0]
    near, far = seq_index // sides, seq_index % sides
    heads = blocks // sides
    total = heads * rows
    wide = sides * span
    lane = lax.broadcasted_iota(jnp.int32, (1, wide), 1)
    within = lane % span
    pos = ((lane // span) * sides + far) * rows + within - cached
    pos = jnp.where(within < cached, -1, pos)
    token = lax.broadcasted_iota(jnp.int32, (total, 1), 0) % rows
    column = lax.broadcasted_iota(jnp.int32, (rows, 128), 1)
    factor = scale * math.log2(math.e)
    logs = jnp.zeros((rows, 128), f32)
    for b in range(sides):
        q = q_ref[b * heads : (b + 1) * heads].reshape(total, width)
        query_pos = (near * sides + b) * rows + token
        top = jnp.full((total, 128), FLOOR, f32)
        for part in range(sides):
            cut = slice(part * span, (part + 1) * span)
            s = lax.dot_general(
                q, kv_ref[part, 0], (((1,), (1,)), ((), ())), preferred_element_type=f32
            )
            s = jnp.where(pos[:, cut] <= query_pos, s, FLOOR)
            s_ref[b % 2, :, cut] = s
            for k in range(span // 128):
                top = jnp.maximum(top, s[:, k * 128 : (k + 1) * 128])
        top = jnp.max(top, axis=1, keepdims=True)
        acc = jnp.zeros((total, width), f32)
        sums = jnp.zeros((total, 128), f32)
        for part in range(sides):
            cut = slice(part * span, (part + 1) * span)
            p = jnp.exp2((s_ref[b % 2, :, cut] - top) * factor)
            for k in range(span // 128):
                sums = sums + p[:, k * 128 : (k + 1) * 128]
            acc = acc + jnp.dot(p.astype(bf16), kv_ref[part, 1], preferred_element_type=f32)
        row_sum = jnp.sum(sums, axis=1, keepdims=True)
        part_out = (acc / row_sum).astype(bf16)
        row_log = top * factor + jnp.log2(row_sum)
        for h in range(heads):
            logs = jnp.where(column == b * heads + h, row_log[h * rows : (h + 1) * rows], logs)
        for k in range(out_ref.shape[0]):
            out_ref[k, b * total : (b + 1) * total, :] = part_out
    logs = logs.T[:blocks]
    first = logs.astype(bf16).astype(f32)
    second = (logs - first).astype(bf16).astype(f32)
    third = logs - first - second
    pieces = jnp.concatenate([first, second, third, jnp.zeros_like(first)], axis=0).astype(bf16)
    for k in range(out_ref.shape[0]):
        out_ref[k, blocks * rows :, :] = pieces


def project(place_ref, got_ref, w_ref, keep_ref, send_ref, *, rows):
    sides, _, width = got_ref.shape
    half = place_ref[1]
    depth = w_ref.shape[0] // sides
    heads = depth // width
    blocks = sides * heads
    base = blocks * rows
    logs = []
    for x in range(sides):
        pieces = got_ref[x, base:, :].astype(f32)
        logs.append(pieces[:blocks] + pieces[blocks : 2 * blocks] + pieces[2 * blocks : 3 * blocks])
    top = functools.reduce(jnp.maximum, logs)
    shares = [jnp.exp2(v - top) for v in logs]
    whole = functools.reduce(jnp.add, shares)
    shares = jnp.concatenate([v / whole for v in shares], axis=0).T
    joined = []
    for b in range(sides):
        line = []
        for h in range(heads):
            k = b * heads + h
            value = jnp.zeros((rows, width), f32)
            for x in range(sides):
                share = shares[:, x * blocks + k : x * blocks + k + 1]
                value = value + share * got_ref[x, k * rows : (k + 1) * rows, :].astype(f32)
            line.append(value.astype(bf16))
        joined.append(jnp.concatenate(line, axis=1))
    x = jnp.concatenate(joined, axis=0)
    for a in range(sides):
        y = jnp.dot(x, w_ref[a * depth : (a + 1) * depth, :], preferred_element_type=f32)
        part = y.shape[1] // 2
        low, high = y[:, :part], y[:, part:]
        keep = jnp.where(half == 0, low, high).astype(bf16)
        send = jnp.where(half == 0, high, low).astype(bf16)
        keep_ref[a * sides : (a + 1) * sides] = keep.reshape(sides, rows, part)
        send_ref[a * sides : (a + 1) * sides] = send.reshape(sides, rows, part)


def add_state(got_ref, packed_ref, out_ref):
    rows = got_ref.shape[1]
    total = packed_ref[0:rows, :].astype(f32)
    for k in range(got_ref.shape[0]):
        total = total + got_ref[k].astype(f32)
    out_ref[0:rows, :] = total.astype(bf16)
    out_ref[rows:, :] = packed_ref[rows:, :]


def dispatch(place_ref, own_ref, other_ref, out_ref, *, capacity):
    half = place_ref[1]
    tokens = own_ref.shape[1]
    own, other = own_ref[0:tokens, :], other_ref[0:tokens, :]
    low = jnp.where(half == 0, own.astype(f32), other.astype(f32)).astype(bf16)
    high = jnp.where(half == 0, other.astype(f32), own.astype(f32)).astype(bf16)
    state = jnp.concatenate([low, high], axis=1)
    chips = out_ref.shape[0] // (2 * capacity)
    ids = own_ref[tokens:, :].astype(f32).astype(jnp.int32)
    before = (
        lax.broadcasted_iota(jnp.int32, (tokens, tokens), 0)
        < lax.broadcasted_iota(jnp.int32, (tokens, tokens), 1)
    ).astype(f32).astype(bf16)
    codes = []
    for member in range(2):
        expert = lax.broadcasted_iota(jnp.int32, (chips, tokens), 0) * 4 + 2 * half + member
        taken = jnp.zeros((chips, tokens), f32)
        for k in range(ids.shape[0]):
            taken = taken + (expert == ids[k : k + 1, :]).astype(f32)
        slot = jnp.dot(taken.astype(bf16), before, preferred_element_type=f32)
        codes.append(jnp.where(taken > 0, slot.astype(jnp.int32) + member * capacity, -1))
    slots = lax.broadcasted_iota(jnp.int32, (chips, 2 * capacity, tokens), 1)
    chosen = (codes[0][:, None, :] == slots) | (codes[1][:, None, :] == slots)
    select = chosen.astype(f32).reshape(chips * 2 * capacity, tokens).astype(bf16)
    out_ref[...] = jnp.dot(select, state, preferred_element_type=f32).astype(bf16)


def gate_up(place_ref, x_ref, gain_ref, *refs, capacity):
    *w_refs, out_ref = refs
    sides, _, slots, depth = x_ref.shape
    near = place_ref[0] // sides
    total = sides * slots
    columns = w_refs[0].shape[-1]
    sums = [jnp.zeros((total, columns), f32)] * 2
    squares = jnp.zeros((total, 1), f32)
    for k in range(sides):
        block = lax.rem(near + sides - k, sides)
        x = x_ref[:, block].reshape(total, depth).astype(f32)
        squares = squares + jnp.sum(x * x, axis=1, keepdims=True)
        scaled = (x * gain_ref[block]).astype(bf16)
        for m in range(2):
            sums[m] = sums[m] + jnp.dot(scaled, w_refs[k][m], preferred_element_type=f32)
    second = lax.broadcasted_iota(jnp.int32, (total, 1), 0) % (2 * capacity) >= capacity
    out_ref[:, :columns] = jnp.where(second, sums[1], sums[0]).astype(bf16)
    high = squares.astype(bf16).astype(f32)
    lane = lax.broadcasted_iota(jnp.int32, (total, 128), 1)
    out_ref[:, columns:] = jnp.where(lane < 64, high, squares - high).astype(bf16)


def activate(got_ref, extra_ref, out_ref, *, features):
    blocks, slots, _ = got_ref.shape

    def total(k):
        value = got_ref[0, :, k * 128 : (k + 1) * 128].astype(f32)
        for j in range(1, blocks):
            value = value + got_ref[j, :, k * 128 : (k + 1) * 128].astype(f32)
        return value

    pieces = total(3)
    squares = pieces[:, 0:1] + pieces[:, 64:65]
    norm = lax.rsqrt(squares / features + 1e-6)
    values = []
    for k in range(3):
        both = total(k) * norm
        values.append(both / (1.0 + jnp.exp(-both)) * pltpu.roll(both, 64, 1))
    part = slots // 2
    left = lax.broadcasted_iota(jnp.int32, (slots, 128), 1) < 64
    full = jnp.where(left, values[0], pltpu.roll(values[1], 64, 1)).astype(bf16)
    rest = jnp.where(left[:part], values[2][:part], pltpu.roll(values[2][part:], 64, 1)).astype(bf16)
    extra = extra_ref[...]
    for k in range(out_ref.shape[0]):
        out_ref[k, 0:slots, :] = full
        out_ref[k, slots : slots + part, :] = rest
        out_ref[k, slots + part :, :] = extra


def combine(place_ref, got_ref, w_in_ref, state_ref, keep_ref, send_ref, x_ref, w_ref, *, capacity):
    half, chip = place_ref[1], place_ref[2]
    pairs = got_ref.shape[0] // 2
    slots = 2 * 2 * capacity
    tokens = state_ref.shape[0]
    width = w_ref.shape[2]
    chips = keep_ref.shape[0]
    size = 2 * tokens
    sides = math.isqrt(got_ref.shape[0])
    part = x_ref.shape[0] // sides
    rest = part // 2
    left = lax.broadcasted_iota(jnp.int32, (rest, 128), 1) < 64
    for y in range(sides):
        w_ref[:, y * 128 : (y + 1) * 128] = w_in_ref[:, y * 192 : y * 192 + 128]
        start = sides * 128 + y * 64
        w_ref[:, start : start + 64] = w_in_ref[:, y * 192 + 128 : (y + 1) * 192]
        for x in range(sides):
            x_ref[x * part : (x + 1) * part, y * 128 : (y + 1) * 128] = got_ref[y * sides + x, :part]
    for x in range(sides):
        for y in range(0, sides, 2):
            a, b = (got_ref[k * sides + x, part : part + rest].astype(f32) for k in (y, y + 1))
            cut = slice((sides + y // 2) * 128, (sides + y // 2 + 1) * 128)
            one = jnp.where(left, a, pltpu.roll(b, 64, 1)).astype(bf16)
            two = jnp.where(left, pltpu.roll(a, 64, 1), b).astype(bf16)
            x_ref[x * part : x * part + rest, cut] = one
            x_ref[x * part + rest : (x + 1) * part, cut] = two
    x = x_ref[...]
    second = lax.broadcasted_iota(jnp.int32, (x.shape[0], 1), 0) % (2 * capacity) >= capacity
    y = jnp.where(
        second,
        jnp.dot(x, w_ref[1], preferred_element_type=f32),
        jnp.dot(x, w_ref[0], preferred_element_type=f32),
    )
    place = lax.broadcasted_iota(jnp.int32, (size, tokens), 0)
    token = (place % tokens // 8) * 8 + place // tokens * 4 + place % 4
    mine = (place % 8 // 4) == chip % 2
    column = lax.broadcasted_iota(jnp.int32, (size, tokens), 1)
    own = jnp.dot(
        ((token == column) & mine).astype(f32).astype(bf16), state_ref[...], preferred_element_type=f32
    )
    slot = lax.broadcasted_iota(jnp.int32, (slots, size), 0) + 1
    for j in range(pairs):
        table = got_ref[2 * j, part + rest :].astype(f32) + got_ref[2 * j + 1, part + rest :].astype(f32)
        table = jnp.concatenate([table[:8], table[8:]], axis=1)
        code = table.astype(jnp.int32)
        hit_a = slot == code[0:1, :]
        hit_b = slot == code[1:2, :]
        weight_a = table[2:3, :] + table[3:4, :] + table[4:5, :]
        weight_b = table[5:6, :] + table[6:7, :] + table[7:8, :]
        weight = jnp.where(hit_a, weight_a, 0.0) + jnp.where(hit_b, weight_b, 0.0)
        weight = jnp.sum(weight, axis=1, keepdims=True)
        rows = (y[j * slots : (j + 1) * slots] * weight).astype(bf16)
        select = (hit_a | hit_b).astype(f32).astype(bf16)
        found = lax.dot_general(select, rows, (((0,), (0,)), ((), ())), preferred_element_type=f32)
        mine = jnp.where(j == chip // 2, own, 0.0)
        found = found + jnp.concatenate(
            [jnp.where(half == 0, mine, 0.0), jnp.where(half == 0, 0.0, mine)], axis=1
        )
        low, high = found[:tokens], found[tokens:]
        keep = jnp.where(half == 0, low, high).astype(bf16)
        send = jnp.where(half == 0, high, low).astype(bf16)
        keep_ref[:, j * 8 : (j + 1) * 8, :] = keep.reshape(chips, 8, width)
        send_ref[:, j * 8 : (j + 1) * 8, :] = send.reshape(chips, 8, width)


def local(
    queries,
    cache,
    new_key_value,
    out_proj,
    residual,
    norm_gain,
    expert_ids,
    gates,
    w_gate_up,
    w_down,
):
    n_seq, n_exp = lax.axis_size("seq"), lax.axis_size("exp")
    n_chip = n_exp // 2
    seq_index, exp_index = lax.axis_index("seq"), lax.axis_index("exp")
    core, chip = exp_index % 2, exp_index // 2
    place = jnp.stack([seq_index, core, chip]).astype(jnp.int32)
    rows, heads, width = queries.shape
    top_k = expert_ids.shape[1]
    features = norm_gain.shape[0]
    members, feature_block, gate_columns = w_gate_up.shape
    hidden_units = w_down.shape[1]
    capacity = 5 * rows * top_k // (4 * members * n_exp)
    swap = [(i, i ^ 1) for i in range(n_exp)]
    chips = [[2 * z + c for z in range(n_chip)] for c in range(2)]
    sides = math.isqrt(n_seq)
    along_x = [[sides * y + x for x in range(sides)] for y in range(sides)]
    along_y = [[sides * y + x for y in range(sides)] for x in range(sides)]

    def spots():
        return np.ndindex(sides, sides, sides, sides, 2)

    def flat(y, x, a, b, c):
        return (sides * y + x) * n_exp + 2 * (sides * a + b) + c

    swap_x = [(flat(y, b, a, x, c), flat(y, x, a, b, c)) for y, x, a, b, c in spots()]
    swap_y = [(flat(y, x, a, b, c), flat(a, x, y, b, c)) for y, x, a, b, c in spots()]

    def over_chips(value):
        return lax.all_to_all(value, "exp", 0, 0, tiled=True, axis_index_groups=chips)

    def over_seq(value, groups=None):
        return lax.all_to_all(value, "seq", 0, 0, tiled=True, axis_index_groups=groups)

    with jax.named_scope("turn_residual"):
        packed = jnp.concatenate([residual, expert_ids.T.astype(bf16)], axis=0)
        turned = lax.ppermute(packed, ("seq", "exp"), swap_x)

    with jax.named_scope("key_values"):
        group = exp_index * heads // (QUERY_HEADS // KEY_VALUE_HEADS)
        own_cache = lax.dynamic_index_in_dim(cache, group, 1, keepdims=False)
        own_fresh = lax.dynamic_index_in_dim(new_key_value, group, 1, keepdims=False)
        own_kv = jnp.concatenate([own_cache, own_fresh], axis=0).transpose(1, 0, 2)
        kv = over_seq(jnp.broadcast_to(own_kv[None], (sides,) + own_kv.shape), along_y)
        q = lax.all_gather(
            queries.transpose(1, 0, 2), "seq", axis=0, tiled=True, axis_index_groups=along_x
        )

    with jax.named_scope("tables"):
        lines = []
        weights = []
        for member in range(2):
            chosen = expert_ids == exp_index * 2 + member
            taken = jnp.sum(chosen.astype(jnp.int32), axis=1)
            slot = jnp.cumsum(taken) - taken
            code = slot + member * capacity + (seq_index % 2) * 2 * capacity + 1
            lines.append(jnp.where(taken > 0, code, 0).astype(f32))
            weight = jnp.sum(jnp.where(chosen, gates, 0.0), axis=1)
            first = lax.reduce_precision(weight, 8, 7)
            second = lax.reduce_precision(weight - first, 8, 7)
            weights += [first, second, weight - first - second]
        table = jnp.stack(lines + weights).reshape(8, n_chip, 2, 1, 4).transpose(0, 2, 1, 3, 4)
        spot = (jnp.arange(2) == seq_index % 2).astype(f32).reshape(1, 1, 1, 2, 1)
        extra = (table * spot).reshape(8, 2 * rows).astype(bf16)
        extra = jnp.concatenate([extra[:, :rows], extra[:, rows:]], axis=0)

    with jax.named_scope("attention"):
        cached = cache.shape[0]
        span = cached + rows
        attended = run(
            functools.partial(attend, rows=rows, cached=cached, scale=1.0 / math.sqrt(width)),
            shape((sides, (sides * heads) * rows + 4 * sides * heads, width)),
            q,
            kv,
            place=place,
            flops=4 * q.size * span * sides,
            moved=kv.size * 2,
            scratch=[pltpu.VMEM((2, heads * rows, sides * span), f32)],
            name="attend",
        )
        columns = lax.all_gather(
            lax.optimization_barrier((out_proj, kv))[0],
            "seq",
            axis=0,
            tiled=True,
            axis_index_groups=along_y,
        )

    with jax.named_scope("projection"):
        part = shape((n_chip, rows, feature_block // 2))
        keep, send = run(
            functools.partial(project, rows=rows),
            [part, part],
            over_seq(attended, along_x),
            columns,
            place=place,
            name="project",
        )
        paired = (keep.astype(f32) + lax.ppermute(send, "exp", swap).astype(f32)).astype(bf16)
        weights = lax.optimization_barrier((w_gate_up, paired))[0]
        weights = weights.reshape(members, feature_block, 2, sides, -1, 64)
        weights = weights.transpose(3, 0, 1, 4, 2, 5).reshape(sides, members, feature_block, -1)
        blocks = []
        for k in range(sides):
            block = lax.dynamic_index_in_dim(weights, (seq_index // sides + k) % sides, 0, False)
            if k:
                ring = [
                    (sides * y + x, sides * ((y + k) % sides) + x)
                    for y in range(sides)
                    for x in range(sides)
                ]
                block = lax.ppermute(block, "seq", ring)
            blocks.append(block)
        gathered, blocks = lax.optimization_barrier((over_chips(paired), blocks))
        own_state = run(
            add_state,
            shape(turned.shape),
            gathered,
            turned,
            name="add_state",
        )
        other_state = lax.ppermute(own_state, "exp", swap)

    with jax.named_scope("gate_up"):
        slots = 2 * capacity
        outgoing = run(
            functools.partial(dispatch, capacity=capacity),
            shape((n_chip * slots, feature_block)),
            own_state,
            other_state,
            place=place,
            name="dispatch",
        )
        incoming = over_chips(outgoing.reshape(n_chip, slots, feature_block))
        incoming = incoming.reshape(1, sides, sides * slots, feature_block)
        incoming = over_seq(jnp.broadcast_to(incoming, (sides,) + incoming.shape[1:]), along_y)
        state = lax.ppermute(own_state[:rows], ("seq", "exp"), swap_y)
        gain = lax.dynamic_index_in_dim(
            norm_gain.reshape(sides, sides, 1, feature_block), seq_index % sides, 1, False
        )
        width = blocks[0].shape[-1] + 128
        partial = run(
            functools.partial(gate_up, capacity=capacity),
            shape((n_seq * slots, width)),
            incoming,
            gain,
            *blocks,
            place=place,
            name="gate_up",
        )
        sums = over_seq(partial.reshape(sides, sides * slots, width), along_x)

    with jax.named_scope("down"):
        quarter = sides * slots
        active = run(
            functools.partial(activate, features=features),
            shape((n_seq, quarter + quarter // 2 + extra.shape[0], 128)),
            sums,
            extra,
            name="activate",
        )
        line = shape((n_chip, n_seq * 4, feature_block))
        keep, send = run(
            functools.partial(combine, capacity=capacity),
            [line, line],
            over_seq(active),
            w_down,
            state,
            place=place,
            scratch=[
                pltpu.VMEM((n_seq * slots, hidden_units), bf16),
                pltpu.VMEM((members, hidden_units, feature_block), bf16),
            ],
            name="combine",
        )

    with jax.named_scope("output"):
        paired = (keep.astype(f32) + lax.ppermute(send, "exp", swap).astype(f32)).astype(bf16)
        mixed = jnp.sum(over_chips(paired).astype(f32), axis=0).astype(bf16)
        mixed = over_seq(mixed.reshape(n_seq, 4, feature_block))
        return mixed.transpose(1, 0, 2).reshape(4, features)


def solution(mesh):
    in_specs = (
        P("seq", "exp", None),
        P("seq", None, None, None),
        P("seq", None, None, None),
        P("exp", "seq"),
        P("seq", "exp"),
        P(),
        P("seq", None),
        P("seq", None),
        P("exp", "seq", None),
        P("exp", None, "seq"),
    )
    out_specs = P(("seq", "exp"), None)
    return jax.shard_map(local, mesh=mesh, in_specs=in_specs, out_specs=out_specs, check_vma=False)
```

```python
import functools
import math

import jax
import jax.numpy as jnp
import numpy as np
from jax import lax
from jax.experimental import pallas as pl
from jax.experimental.pallas import tpu as pltpu
from jax.sharding import PartitionSpec as P

QUERY_HEADS = 64
KEY_VALUE_HEADS = 4
FLOOR = -1e30
VMEM_BYTES = 56 * 1024 * 1024
f32 = jnp.float32
bf16 = jnp.bfloat16


def run(body, out_shape, *operands, place=None, flops=0, moved=0, scratch=(), name=None):
    vmem = pl.BlockSpec(memory_space=pltpu.VMEM)
    smem = pl.BlockSpec(memory_space=pltpu.SMEM)
    placed = [] if place is None else [place]
    return pl.pallas_call(
        body,
        out_shape=out_shape,
        in_specs=[smem] * len(placed) + [vmem] * len(operands),
        out_specs=jax.tree.map(lambda _: vmem, out_shape),
        scratch_shapes=list(scratch),
        compiler_params=pltpu.CompilerParams(vmem_limit_bytes=VMEM_BYTES),
        cost_estimate=pl.CostEstimate(flops=flops, bytes_accessed=moved, transcendentals=0),
        name=name,
    )(*placed, *operands)


def shape(dims, dtype=bf16):
    return jax.ShapeDtypeStruct(dims, dtype)


def attend(place_ref, q_ref, kv_ref, out_ref, s_ref, *, rows, cached, scale):
    sides, _, span, width = kv_ref.shape
    blocks = q_ref.shape[0]
    seq_index = place_ref[0]
    near, far = seq_index // sides, seq_index % sides
    heads = blocks // sides
    total = heads * rows
    wide = sides * span
    lane = lax.broadcasted_iota(jnp.int32, (1, wide), 1)
    within = lane % span
    pos = ((lane // span) * sides + far) * rows + within - cached
    pos = jnp.where(within < cached, -1, pos)
    token = lax.broadcasted_iota(jnp.int32, (total, 1), 0) % rows
    column = lax.broadcasted_iota(jnp.int32, (rows, 128), 1)
    factor = scale * math.log2(math.e)
    logs = jnp.zeros((rows, 128), f32)
    for b in range(sides):
        q = q_ref[b * heads : (b + 1) * heads].reshape(total, width)
        query_pos = (near * sides + b) * rows + token
        top = jnp.full((total, 128), FLOOR, f32)
        for part in range(sides):
            cut = slice(part * span, (part + 1) * span)
            s = lax.dot_general(
                q, kv_ref[part, 0], (((1,), (1,)), ((), ())), preferred_element_type=f32
            )
            s = jnp.where(pos[:, cut] <= query_pos, s, FLOOR)
            s_ref[b % 2, :, cut] = s
            for k in range(span // 128):
                top = jnp.maximum(top, s[:, k * 128 : (k + 1) * 128])
        top = jnp.max(top, axis=1, keepdims=True)
        acc = jnp.zeros((total, width), f32)
        sums = jnp.zeros((total, 128), f32)
        for part in range(sides):
            cut = slice(part * span, (part + 1) * span)
            p = jnp.exp2((s_ref[b % 2, :, cut] - top) * factor)
            for k in range(span // 128):
                sums = sums + p[:, k * 128 : (k + 1) * 128]
            acc = acc + jnp.dot(p.astype(bf16), kv_ref[part, 1], preferred_element_type=f32)
        row_sum = jnp.sum(sums, axis=1, keepdims=True)
        part_out = (acc / row_sum).astype(bf16)
        row_log = top * factor + jnp.log2(row_sum)
        for h in range(heads):
            logs = jnp.where(column == b * heads + h, row_log[h * rows : (h + 1) * rows], logs)
        for k in range(out_ref.shape[0]):
            out_ref[k, b * total : (b + 1) * total, :] = part_out
    logs = logs.T[:blocks]
    first = logs.astype(bf16).astype(f32)
    second = (logs - first).astype(bf16).astype(f32)
    third = logs - first - second
    pieces = jnp.concatenate([first, second, third, jnp.zeros_like(first)], axis=0).astype(bf16)
    for k in range(out_ref.shape[0]):
        out_ref[k, blocks * rows :, :] = pieces


def project(place_ref, got_ref, w_ref, keep_ref, send_ref, *, rows):
    sides, _, width = got_ref.shape
    half = place_ref[1]
    depth = w_ref.shape[0] // sides
    heads = depth // width
    blocks = sides * heads
    base = blocks * rows
    logs = []
    for x in range(sides):
        pieces = got_ref[x, base:, :].astype(f32)
        logs.append(pieces[:blocks] + pieces[blocks : 2 * blocks] + pieces[2 * blocks : 3 * blocks])
    top = functools.reduce(jnp.maximum, logs)
    shares = [jnp.exp2(v - top) for v in logs]
    whole = functools.reduce(jnp.add, shares)
    shares = jnp.concatenate([v / whole for v in shares], axis=0).T
    joined = []
    for b in range(sides):
        line = []
        for h in range(heads):
            k = b * heads + h
            value = jnp.zeros((rows, width), f32)
            for x in range(sides):
                share = shares[:, x * blocks + k : x * blocks + k + 1]
                value = value + share * got_ref[x, k * rows : (k + 1) * rows, :].astype(f32)
            line.append(value.astype(bf16))
        joined.append(jnp.concatenate(line, axis=1))
    x = jnp.concatenate(joined, axis=0)
    for a in range(sides):
        y = jnp.dot(x, w_ref[a * depth : (a + 1) * depth, :], preferred_element_type=f32)
        part = y.shape[1] // 2
        low, high = y[:, :part], y[:, part:]
        keep = jnp.where(half == 0, low, high).astype(bf16)
        send = jnp.where(half == 0, high, low).astype(bf16)
        keep_ref[a * sides : (a + 1) * sides] = keep.reshape(sides, rows, part)
        send_ref[a * sides : (a + 1) * sides] = send.reshape(sides, rows, part)


def add_state(got_ref, packed_ref, out_ref):
    rows = got_ref.shape[1]
    total = packed_ref[0:rows, :].astype(f32)
    for k in range(got_ref.shape[0]):
        total = total + got_ref[k].astype(f32)
    out_ref[0:rows, :] = total.astype(bf16)
    out_ref[rows:, :] = packed_ref[rows:, :]


def dispatch(place_ref, own_ref, other_ref, out_ref, *, capacity):
    half = place_ref[1]
    tokens = own_ref.shape[1]
    own, other = own_ref[0:tokens, :], other_ref[0:tokens, :]
    low = jnp.where(half == 0, own.astype(f32), other.astype(f32)).astype(bf16)
    high = jnp.where(half == 0, other.astype(f32), own.astype(f32)).astype(bf16)
    state = jnp.concatenate([low, high], axis=1)
    chips, size, _ = out_ref.shape
    ids = own_ref[tokens:, :].astype(f32).astype(jnp.int32)
    before = (
        lax.broadcasted_iota(jnp.int32, (tokens, tokens), 0)
        < lax.broadcasted_iota(jnp.int32, (tokens, tokens), 1)
    ).astype(f32).astype(bf16)
    codes = []
    for member in range(2):
        expert = lax.broadcasted_iota(jnp.int32, (chips, tokens), 0) * 4 + 2 * half + member
        taken = jnp.zeros((chips, tokens), f32)
        for k in range(ids.shape[0]):
            taken = taken + (expert == ids[k : k + 1, :]).astype(f32)
        slot = jnp.dot(taken.astype(bf16), before, preferred_element_type=f32)
        codes.append(jnp.where(taken > 0, slot.astype(jnp.int32) + member * capacity, -1))
    slots = lax.broadcasted_iota(jnp.int32, (chips, size, tokens), 1)
    chosen = (codes[0][:, None, :] == slots) | (codes[1][:, None, :] == slots)
    place = lax.broadcasted_iota(jnp.int32, (chips, size, tokens), 0) * 8 + 4 * half
    own = slots - 2 * capacity
    token = lax.broadcasted_iota(jnp.int32, (chips, size, tokens), 2)
    chosen = chosen | ((own >= 0) & (own < 4) & (token == place + own))
    select = chosen.astype(f32).reshape(chips * size, tokens).astype(bf16)
    rows = jnp.dot(select, state, preferred_element_type=f32)
    out_ref[...] = rows.astype(bf16).reshape(out_ref.shape)


def split_columns(place_ref, w_ref, own_ref, next_ref, prev_ref, all_ref):
    sides = all_ref.shape[0]
    near = place_ref[0] // sides
    members, depth, columns = w_ref.shape
    left = lax.broadcasted_iota(jnp.int32, (depth, 128), 1) < 64
    for m in range(members):
        for q in range(columns // 128):
            cut = slice(q // 2 * 128, (q // 2 + 1) * 128)
            gate = w_ref[m, :, cut].astype(f32)
            up = w_ref[m, :, columns // 2 + cut.start : columns // 2 + cut.stop].astype(f32)
            if q % 2:
                gate = pltpu.roll(gate, 64, 1)
            else:
                up = pltpu.roll(up, 64, 1)
            per = columns // 128 // sides
            out = slice(q % per * 128, (q % per + 1) * 128)
            all_ref[q // per, m, :, out] = jnp.where(left, gate, up).astype(bf16)
    far = lax.rem(near + 2, sides)
    own_ref[...] = all_ref[near]
    for ref, step, m in ((next_ref, 1, 0), (prev_ref, sides - 1, 1)):
        ref[0:2] = all_ref[lax.rem(near + step, sides)]
        ref[2] = all_ref[far, m]


def gate_up(place_ref, x_ref, state_ref, gain_ref, own_ref, prev_ref, next_ref, opp_ref, opp2_ref, out_ref, *, capacity):
    w_refs = (
        (own_ref.at[0], own_ref.at[1]),
        (prev_ref.at[0], prev_ref.at[1]),
        (opp_ref, opp2_ref),
        (next_ref.at[0], next_ref.at[1]),
    )
    sides, _, slots, depth = x_ref.shape
    near = place_ref[0] // sides
    total = sides * slots
    columns = own_ref.shape[-1]
    sums = [jnp.zeros((total, columns), f32)] * 2
    squares = jnp.zeros((total, 1), f32)
    for k in range(sides):
        block = lax.rem(near + sides - k, sides)
        x = x_ref[:, block].reshape(total, depth).astype(f32)
        squares = squares + jnp.sum(x * x, axis=1, keepdims=True)
        scaled = (x * gain_ref[block]).astype(bf16)
        for m in range(2):
            sums[m] = sums[m] + jnp.dot(scaled, w_refs[k][m][...], preferred_element_type=f32)
    second = lax.broadcasted_iota(jnp.int32, (total, 1), 0) % (2 * capacity) >= capacity
    partial = jnp.where(second, sums[1], sums[0])
    high = squares.astype(bf16).astype(f32)
    lane = lax.broadcasted_iota(jnp.int32, (total, 128), 1)
    pieces = jnp.where(lane < 64, high, squares - high)
    size = 2 * capacity
    for a in range(sides):
        for b in range(sides):
            cut = slice((a * sides + b) * size, (a * sides + b + 1) * size)
            state = state_ref[a, b].astype(f32)
            slot_rows = jnp.concatenate([partial[cut], pieces[cut]], axis=1)
            state = jnp.concatenate([state, jnp.zeros_like(state)], axis=1)
            out_ref[b, a] = jnp.concatenate([slot_rows, state], axis=0).astype(bf16)


def activate(got_ref, extra_ref, out_ref, state_ref, *, features):
    blocks, lines, size, _ = got_ref.shape
    extra_rows = 8
    slots = lines * (size - extra_rows)
    width = state_ref.shape[1] // (blocks * lines)
    for a in range(lines):
        for x in range(blocks):
            start = (a * blocks + x) * width
            state = got_ref[x, a, :, :width].astype(f32)[size - extra_rows :]
            state_ref[:, start : start + width] = state

    def total(k):
        value = got_ref[0, :, :, k * 128 : (k + 1) * 128].astype(f32)
        for j in range(1, blocks):
            value = value + got_ref[j, :, :, k * 128 : (k + 1) * 128].astype(f32)
        return value[:, : size - extra_rows].reshape(slots, 128)

    pieces = total(3)
    squares = pieces[:, 0:1] + pieces[:, 64:65]
    norm = lax.rsqrt(squares / features + 1e-6)
    values = []
    for k in range(3):
        both = total(k) * norm
        values.append(both / (1.0 + jnp.exp(-both)) * pltpu.roll(both, 64, 1))
    part = slots // 2
    left = lax.broadcasted_iota(jnp.int32, (slots, 128), 1) < 64
    full = jnp.where(left, values[0], pltpu.roll(values[1], 64, 1)).astype(bf16)
    rest = jnp.where(left[:part], values[2][:part], pltpu.roll(values[2][part:], 64, 1)).astype(bf16)
    extra = extra_ref[...]
    for k in range(out_ref.shape[0]):
        out_ref[k, 0:slots, :] = full
        out_ref[k, slots : slots + part, :] = rest
        out_ref[k, slots + part :, :] = extra


def combine(
    place_ref,
    got_ref,
    own_ref,
    prev_ref,
    next_ref,
    opp_ref,
    opp2_ref,
    out_ref,
    x_ref,
    w_ref,
    *,
    capacity,
):
    w_refs = (
        (own_ref.at[0], own_ref.at[1]),
        (prev_ref.at[0], prev_ref.at[1]),
        (opp_ref, opp2_ref),
        (next_ref.at[0], next_ref.at[1]),
    )
    sides = got_ref.shape[0]
    far = place_ref[0] % sides
    slots = x_ref.shape[0]
    rest = slots // 2
    width = w_ref.shape[2]
    size = got_ref.shape[2] * sides
    left = lax.broadcasted_iota(jnp.int32, (rest, 128), 1) < 64
    for y in range(sides):
        x_ref[:, y * 128 : (y + 1) * 128] = got_ref[y, :slots]
    for y in range(0, sides, 2):
        a, b = (got_ref[k, slots : slots + rest].astype(f32) for k in (y, y + 1))
        cut = slice((sides + y // 2) * 128, (sides + y // 2 + 1) * 128)
        x_ref[:rest, cut] = jnp.where(left, a, pltpu.roll(b, 64, 1)).astype(bf16)
        x_ref[rest:, cut] = jnp.where(left, pltpu.roll(a, 64, 1), b).astype(bf16)
    x = x_ref[...]

    table = got_ref[0, slots + rest :].astype(f32)
    for y in range(1, sides):
        table = table + got_ref[y, slots + rest :].astype(f32)
    table = jnp.concatenate([table[k * 8 : (k + 1) * 8] for k in range(sides)], axis=1)
    code = table.astype(jnp.int32)
    slot = lax.broadcasted_iota(jnp.int32, (slots, size), 0) + 1
    hit_a = slot == code[0:1, :]
    hit_b = slot == code[1:2, :]
    weight_a = table[2:3, :] + table[3:4, :] + table[4:5, :]
    weight_b = table[5:6, :] + table[6:7, :] + table[7:8, :]
    weight = jnp.where(hit_a, weight_a, 0.0) + jnp.where(hit_b, weight_b, 0.0)
    weight = jnp.sum(weight, axis=1, keepdims=True)
    select = (hit_a | hit_b).astype(f32).T.astype(bf16)

    second = lax.broadcasted_iota(jnp.int32, (slots, 1), 0) % (2 * capacity) >= capacity
    for k in range(sides):
        block = lax.rem(far + sides - k, sides)
        for m in range(2):
            for y in range(sides):
                w_ref[m, y * 128 : (y + 1) * 128] = w_refs[k][m][y * 192 : y * 192 + 128]
                start = sides * 128 + y * 64
                w_ref[m, start : start + 64] = w_refs[k][m][y * 192 + 128 : (y + 1) * 192]
        result = jnp.where(
            second,
            jnp.dot(x, w_ref[1], preferred_element_type=f32),
            jnp.dot(x, w_ref[0], preferred_element_type=f32),
        )
        found = jnp.dot(select, (result * weight).astype(bf16), preferred_element_type=f32)
        start = pl.multiple_of(block * width, width)
        out_ref[:, :, :, pl.ds(start, width)] = found.astype(bf16).reshape(sides, -1, 16, width)


def local(
    queries,
    cache,
    new_key_value,
    out_proj,
    residual,
    norm_gain,
    expert_ids,
    gates,
    w_gate_up,
    w_down,
):
    n_seq, n_exp = lax.axis_size("seq"), lax.axis_size("exp")
    n_chip = n_exp // 2
    seq_index, exp_index = lax.axis_index("seq"), lax.axis_index("exp")
    core, chip = exp_index % 2, exp_index // 2
    place = jnp.stack([seq_index, core, chip]).astype(jnp.int32)
    rows, heads, width = queries.shape
    top_k = expert_ids.shape[1]
    features = norm_gain.shape[0]
    members, feature_block, gate_columns = w_gate_up.shape
    hidden_units = w_down.shape[1]
    capacity = 5 * rows * top_k // (4 * members * n_exp)
    swap = [(i, i ^ 1) for i in range(n_exp)]
    near = [[4 * p + i for i in range(4)] for p in range(n_chip // 2)]
    far = [[4 * p + i for p in range(n_chip // 2)] for i in range(4)]
    chips = [[2 * z + c for z in range(n_chip)] for c in range(2)]
    sides = math.isqrt(n_seq)
    along_x = [[sides * y + x for x in range(sides)] for y in range(sides)]
    along_y = [[sides * y + x for y in range(sides)] for x in range(sides)]

    def spots():
        return np.ndindex(sides, sides, sides, sides, 2)

    def flat(y, x, a, b, c):
        return (sides * y + x) * n_exp + 2 * (sides * a + b) + c

    swap_x = [(flat(y, b, a, x, c), flat(y, x, a, b, c)) for y, x, a, b, c in spots()]

    def over_chips(value):
        return lax.all_to_all(value, "exp", 0, 0, tiled=True, axis_index_groups=chips)

    def over_seq(value, groups):
        return lax.all_to_all(value, "seq", 0, 0, tiled=True, axis_index_groups=groups)

    def sum_near(value):
        value = lax.all_to_all(value, "exp", 0, 0, tiled=True, axis_index_groups=near)
        return jnp.sum(value.astype(f32), axis=0).astype(bf16)

    def over_far(value):
        return lax.all_to_all(value, "exp", 0, 0, tiled=True, axis_index_groups=far)

    shift_y, shift_x = {}, {}
    for k in (1, -1):
        shift_y[k] = [
            (sides * y + x, sides * ((y + k) % sides) + x) for y in range(sides) for x in range(sides)
        ]
        shift_x[k] = [
            (sides * y + x, sides * y + (x + k) % sides) for y in range(sides) for x in range(sides)
        ]

    with jax.named_scope("turn_residual"):
        packed = jnp.concatenate([residual, expert_ids.T.astype(bf16)], axis=0)
        turned = lax.ppermute(packed, ("seq", "exp"), swap_x)

    with jax.named_scope("key_values"):
        group = exp_index * heads // (QUERY_HEADS // KEY_VALUE_HEADS)
        own_cache = lax.dynamic_index_in_dim(cache, group, 1, keepdims=False)
        own_fresh = lax.dynamic_index_in_dim(new_key_value, group, 1, keepdims=False)
        own_kv = jnp.concatenate([own_cache, own_fresh], axis=0).transpose(1, 0, 2)
        kv = over_seq(jnp.broadcast_to(own_kv[None], (sides,) + own_kv.shape), along_y)
        q = lax.all_gather(
            queries.transpose(1, 0, 2), "seq", axis=0, tiled=True, axis_index_groups=along_x
        )

    with jax.named_scope("attention"):
        cached = cache.shape[0]
        span = cached + rows
        attended = run(
            functools.partial(attend, rows=rows, cached=cached, scale=1.0 / math.sqrt(width)),
            shape((sides, (sides * heads) * rows + 4 * sides * heads, width)),
            q,
            kv,
            place=place,
            flops=4 * q.size * span * sides,
            moved=kv.size * 2,
            scratch=[pltpu.VMEM((2, heads * rows, sides * span), f32)],
            name="attend",
        )
        columns = lax.all_gather(
            lax.optimization_barrier((out_proj, kv))[0],
            "seq",
            axis=0,
            tiled=True,
            axis_index_groups=along_y,
        )

    with jax.named_scope("projection"):
        part = shape((n_chip, rows, feature_block // 2))
        keep, send = run(
            functools.partial(project, rows=rows),
            [part, part],
            over_seq(attended, along_x),
            columns,
            place=place,
            name="project",
        )
        paired = (keep.astype(f32) + lax.ppermute(send, "exp", swap).astype(f32)).astype(bf16)
        weights, w_out, paired = lax.optimization_barrier((w_gate_up, w_down, paired))
        piece = (members, feature_block, gate_columns // sides)
        longer = (members + 1,) + piece[1:]
        w_own, w_next, w_prev = run(
            split_columns,
            [shape(piece), shape(longer), shape(longer)],
            weights,
            place=place,
            scratch=[pltpu.VMEM((sides,) + piece, bf16)],
            name="split_columns",
        )
        near_y = (lax.ppermute(w_next, "seq", shift_y[1]), lax.ppermute(w_prev, "seq", shift_y[-1]))
        near_x = (lax.ppermute(w_out, "seq", shift_x[1]), lax.ppermute(w_out, "seq", shift_x[-1]))
        gathered, near_y, near_x = lax.optimization_barrier((over_chips(paired), near_y, near_x))
        own_state = run(
            add_state,
            shape(turned.shape),
            gathered,
            turned,
            name="add_state",
        )
        other_state = lax.ppermute(own_state, "exp", swap)

    with jax.named_scope("gate_up"):
        slots = 2 * capacity
        size = slots + 8
        outgoing = run(
            functools.partial(dispatch, capacity=capacity),
            shape((n_chip, size, feature_block)),
            own_state,
            other_state,
            place=place,
            name="dispatch",
        )
        incoming = over_chips(outgoing)
        far_y = (
            lax.ppermute(near_y[0][members], "seq", shift_y[1]),
            lax.ppermute(near_y[1][members], "seq", shift_y[-1]),
        )
        far_x = (
            lax.ppermute(near_x[0][0], "seq", shift_x[1]),
            lax.ppermute(near_x[1][1], "seq", shift_x[-1]),
        )
        incoming, far_x, far_y = lax.optimization_barrier((incoming, far_x, far_y))
        incoming = incoming.reshape(sides, sides, size, feature_block)
        state = incoming[:, :, slots:]
        incoming = incoming[:, :, :slots].reshape(1, sides, sides * slots, feature_block)
        incoming = over_seq(jnp.broadcast_to(incoming, (sides,) + incoming.shape[1:]), along_y)
        gain = lax.dynamic_index_in_dim(
            norm_gain.reshape(sides, sides, 1, feature_block), seq_index % sides, 1, False
        )
        width = piece[-1] + 128
        partial = run(
            functools.partial(gate_up, capacity=capacity),
            shape((sides, sides, size, width)),
            incoming,
            state,
            gain,
            w_own,
            *near_y,
            *far_y,
            place=place,
            name="gate_up",
        )
    with jax.named_scope("tables"):
        expert_ids, gates, partial = lax.optimization_barrier((expert_ids, gates, partial))
        lines = []
        weights = []
        for member in range(2):
            chosen = expert_ids == exp_index * 2 + member
            taken = jnp.sum(chosen.astype(jnp.int32), axis=1)
            slot = jnp.cumsum(taken) - taken
            code = slot + member * capacity + (seq_index // sides) * 2 * capacity + 1
            lines.append(jnp.where(taken > 0, code, 0).astype(f32))
            weight = jnp.sum(jnp.where(chosen, gates, 0.0), axis=1)
            first = lax.reduce_precision(weight, 8, 7)
            second = lax.reduce_precision(weight - first, 8, 7)
            weights += [first, second, weight - first - second]
        table = jnp.stack(lines + weights).reshape(8, n_chip // 2, 2, 2, 1, 4)
        spot = (jnp.arange(sides) == seq_index // sides).astype(f32).reshape(1, 1, 1, 1, sides, 1)
        table = (table * spot).transpose(2, 3, 0, 1, 4, 5)
        extra = table.reshape(4 * 8, rows).astype(bf16)

    with jax.named_scope("down"):
        quarter = sides * slots
        sums = over_seq(partial, along_x)
        active, state = run(
            functools.partial(activate, features=features),
            [shape((sides, quarter + quarter // 2 + extra.shape[0], 128)), shape((8, features), f32)],
            sums,
            extra,
            name="activate",
        )
        line = 4 * sides
        partial = run(
            functools.partial(combine, capacity=capacity),
            shape((4, n_chip // 2, line, sides * feature_block)),
            over_seq(active, along_y),
            w_down,
            *near_x,
            *far_x,
            place=place,
            scratch=[
                pltpu.VMEM((quarter, hidden_units), bf16),
                pltpu.VMEM((members, hidden_units, feature_block), bf16),
            ],
            name="combine",
        )

    with jax.named_scope("output"):
        gathered = over_far(sum_near(partial))
        mixed = jnp.sum(gathered.astype(f32), axis=0).astype(bf16)
        mixed = over_seq(mixed.reshape(sides, 4, sides * feature_block), along_y)
        mixed = mixed.transpose(1, 0, 2).reshape(4, features)
        return (state[:4] + mixed.astype(f32)).astype(bf16)


def solution(mesh):
    in_specs = (
        P("seq", "exp", None),
        P("seq", None, None, None),
        P("seq", None, None, None),
        P("exp", "seq"),
        P("seq", "exp"),
        P(),
        P("seq", None),
        P("seq", None),
        P("exp", "seq", None),
        P("exp", None, "seq"),
    )
    out_specs = P(("seq", "exp"), None)
    return jax.shard_map(local, mesh=mesh, in_specs=in_specs, out_specs=out_specs, check_vma=False)
```

```python
import functools
import math

import jax
import jax.numpy as jnp
import numpy as np
from jax import lax
from jax.experimental import pallas as pl
from jax.experimental.pallas import tpu as pltpu
from jax.sharding import PartitionSpec as P

QUERY_HEADS = 64
KEY_VALUE_HEADS = 4
FLOOR = -1e30
f32 = jnp.float32
bf16 = jnp.bfloat16


def run(body, out_shape, *operands, place=None, left=(), room=16, flops=0, moved=0, scratch=(), name=None):
    vmem = pl.BlockSpec(memory_space=pltpu.VMEM)
    spaces = [
        pl.BlockSpec(memory_space=pl.ANY) if i in left else vmem for i in range(len(operands))
    ]
    smem = pl.BlockSpec(memory_space=pltpu.SMEM)
    placed = [] if place is None else [place]
    return pl.pallas_call(
        body,
        out_shape=out_shape,
        in_specs=[smem] * len(placed) + spaces,
        out_specs=jax.tree.map(lambda _: vmem, out_shape),
        scratch_shapes=list(scratch),
        compiler_params=pltpu.CompilerParams(vmem_limit_bytes=room * 1024 * 1024),
        cost_estimate=pl.CostEstimate(flops=flops, bytes_accessed=moved, transcendentals=0),
        name=name,
    )(*placed, *operands)


def shape(dims, dtype=bf16):
    return jax.ShapeDtypeStruct(dims, dtype)


def attend(place_ref, q_ref, kv_ref, out_ref, s_ref, *, rows, cached, scale):
    sides, _, span, width = kv_ref.shape
    blocks = q_ref.shape[0]
    seq_index = place_ref[0]
    near, far = seq_index // sides, seq_index % sides
    heads = blocks // sides
    total = heads * rows
    lane = lax.broadcasted_iota(jnp.int32, (1, rows), 1)
    pos = [(part * sides + far) * rows + lane for part in range(sides)]
    token = lax.broadcasted_iota(jnp.int32, (total, 1), 0) % rows
    column = lax.broadcasted_iota(jnp.int32, (rows, 128), 1)
    factor = scale * math.log2(math.e)
    logs = jnp.zeros((rows, 128), f32)
    for b in range(sides):
        q = q_ref[b * heads : (b + 1) * heads].reshape(total, width)
        query_pos = (near * sides + b) * rows + token
        top = jnp.full((total, 128), FLOOR, f32)
        for part in range(sides):
            s = lax.dot_general(
                q, kv_ref[part, 0], (((1,), (1,)), ((), ())), preferred_element_type=f32
            )
            fresh = jnp.where(pos[part] <= query_pos, s[:, cached:], FLOOR)
            s_ref[b % 2, :, part * span : part * span + cached] = s[:, :cached]
            s_ref[b % 2, :, part * span + cached : (part + 1) * span] = fresh
            for k in range(cached // 128):
                top = jnp.maximum(top, s[:, k * 128 : (k + 1) * 128])
            for k in range(rows // 128):
                top = jnp.maximum(top, fresh[:, k * 128 : (k + 1) * 128])
        top = jnp.max(top, axis=1, keepdims=True)
        acc = jnp.zeros((total, width), f32)
        sums = jnp.zeros((total, 128), f32)
        for part in range(sides):
            cut = slice(part * span, (part + 1) * span)
            p = jnp.exp2((s_ref[b % 2, :, cut] - top) * factor)
            for k in range(span // 128):
                sums = sums + p[:, k * 128 : (k + 1) * 128]
            acc = acc + jnp.dot(p.astype(bf16), kv_ref[part, 1], preferred_element_type=f32)
        row_sum = jnp.sum(sums, axis=1, keepdims=True)
        part_out = (acc / row_sum).astype(bf16)
        row_log = top * factor + jnp.log2(row_sum)
        for h in range(heads):
            logs = jnp.where(column == b * heads + h, row_log[h * rows : (h + 1) * rows], logs)
        for k in range(out_ref.shape[0]):
            out_ref[k, b * total : (b + 1) * total, :] = part_out
    logs = logs.T[:blocks]
    first = logs.astype(bf16).astype(f32)
    second = (logs - first).astype(bf16).astype(f32)
    third = logs - first - second
    pieces = jnp.concatenate([first, second, third, jnp.zeros_like(first)], axis=0).astype(bf16)
    for k in range(out_ref.shape[0]):
        out_ref[k, blocks * rows :, :] = pieces


def project(place_ref, got_ref, w_ref, keep_ref, send_ref, *, rows):
    sides, _, width = got_ref.shape
    half = place_ref[1]
    depth = w_ref.shape[0] // sides
    heads = depth // width
    blocks = sides * heads
    base = blocks * rows
    logs = []
    for x in range(sides):
        pieces = got_ref[x, base:, :].astype(f32)
        logs.append(pieces[:blocks] + pieces[blocks : 2 * blocks] + pieces[2 * blocks : 3 * blocks])
    top = functools.reduce(jnp.maximum, logs)
    shares = [jnp.exp2(v - top) for v in logs]
    whole = functools.reduce(jnp.add, shares)
    shares = jnp.concatenate([v / whole for v in shares], axis=0).T
    joined = []
    for b in range(sides):
        line = []
        for h in range(heads):
            k = b * heads + h
            value = jnp.zeros((rows, width), f32)
            for x in range(sides):
                share = shares[:, x * blocks + k : x * blocks + k + 1]
                value = value + share * got_ref[x, k * rows : (k + 1) * rows, :].astype(f32)
            line.append(value.astype(bf16))
        joined.append(jnp.concatenate(line, axis=1))
    x = jnp.concatenate(joined, axis=0)
    for a in range(sides):
        y = jnp.dot(x, w_ref[a * depth : (a + 1) * depth, :], preferred_element_type=f32)
        part = y.shape[1] // 2
        low, high = y[:, :part], y[:, part:]
        keep = jnp.where(half == 0, low, high).astype(bf16)
        send = jnp.where(half == 0, high, low).astype(bf16)
        keep_ref[a * sides : (a + 1) * sides] = keep.reshape(sides, rows, part)
        send_ref[a * sides : (a + 1) * sides] = send.reshape(sides, rows, part)


def add_state(got_ref, packed_ref, out_ref):
    rows = got_ref.shape[1]
    total = packed_ref[0:rows, :].astype(f32)
    for k in range(got_ref.shape[0]):
        total = total + got_ref[k].astype(f32)
    out_ref[0:rows, :] = total.astype(bf16)
    out_ref[rows:, :] = packed_ref[rows:, :]


def dispatch(place_ref, own_ref, other_ref, out_ref, *, capacity):
    half = place_ref[1]
    tokens = own_ref.shape[1]
    own, other = own_ref[0:tokens, :], other_ref[0:tokens, :]
    low = jnp.where(half == 0, own.astype(f32), other.astype(f32)).astype(bf16)
    high = jnp.where(half == 0, other.astype(f32), own.astype(f32)).astype(bf16)
    state = jnp.concatenate([low, high], axis=1)
    chips, size, _ = out_ref.shape
    ids = own_ref[tokens:, :].astype(f32).astype(jnp.int32)
    before = (
        lax.broadcasted_iota(jnp.int32, (tokens, tokens), 0)
        < lax.broadcasted_iota(jnp.int32, (tokens, tokens), 1)
    ).astype(f32).astype(bf16)
    codes = []
    for member in range(2):
        expert = lax.broadcasted_iota(jnp.int32, (chips, tokens), 0) * 4 + 2 * half + member
        taken = jnp.zeros((chips, tokens), f32)
        for k in range(ids.shape[0]):
            taken = taken + (expert == ids[k : k + 1, :]).astype(f32)
        slot = jnp.dot(taken.astype(bf16), before, preferred_element_type=f32)
        codes.append(jnp.where(taken > 0, slot.astype(jnp.int32) + member * capacity, -1))
    slots = lax.broadcasted_iota(jnp.int32, (chips, size, tokens), 1)
    chosen = (codes[0][:, None, :] == slots) | (codes[1][:, None, :] == slots)
    place = lax.broadcasted_iota(jnp.int32, (chips, size, tokens), 0) * 8 + 4 * half
    own = slots - 2 * capacity
    token = lax.broadcasted_iota(jnp.int32, (chips, size, tokens), 2)
    chosen = chosen | ((own >= 0) & (own < 4) & (token == place + own))
    select = chosen.astype(f32).reshape(chips * size, tokens).astype(bf16)
    rows = jnp.dot(select, state, preferred_element_type=f32)
    out_ref[...] = rows.astype(bf16).reshape(out_ref.shape)


def split_columns(place_ref, w_in_ref, own_ref, next_ref, prev_ref, all_ref, w_ref, sem):
    copy = pltpu.make_async_copy(w_in_ref, w_ref, sem)
    copy.start()
    copy.wait()
    sides = all_ref.shape[0]
    near = place_ref[0] // sides
    members, depth, columns = w_ref.shape
    left = lax.broadcasted_iota(jnp.int32, (depth, 128), 1) < 64
    for m in range(members):
        for q in range(columns // 128):
            cut = slice(q // 2 * 128, (q // 2 + 1) * 128)
            gate = w_ref[m, :, cut].astype(f32)
            up = w_ref[m, :, columns // 2 + cut.start : columns // 2 + cut.stop].astype(f32)
            if q % 2:
                gate = pltpu.roll(gate, 64, 1)
            else:
                up = pltpu.roll(up, 64, 1)
            per = columns // 128 // sides
            out = slice(q % per * 128, (q % per + 1) * 128)
            all_ref[q // per, m, :, out] = jnp.where(left, gate, up).astype(bf16)
    far = lax.rem(near + 2, sides)
    own_ref[...] = all_ref[near]
    for ref, step, m in ((next_ref, 1, 0), (prev_ref, sides - 1, 1)):
        ref[0:2] = all_ref[lax.rem(near + step, sides)]
        ref[2] = all_ref[far, m]


def gate_up(place_ref, x_ref, state_ref, gain_ref, own_ref, prev_ref, next_ref, opp_ref, opp2_ref, out_ref, scaled_ref, weight_ref, sems, *, capacity):
    sides, _, slots, depth = x_ref.shape
    parts = (
        (own_ref, weight_ref.at[:, 0:depth]),
        (prev_ref.at[0:2], weight_ref.at[:, depth : 2 * depth]),
        (opp_ref, weight_ref.at[0, 2 * depth : 3 * depth]),
        (opp2_ref, weight_ref.at[1, 2 * depth : 3 * depth]),
        (next_ref.at[0:2], weight_ref.at[:, 3 * depth : 4 * depth]),
    )
    copies = [pltpu.make_async_copy(a, b, sems.at[k]) for k, (a, b) in enumerate(parts)]
    for copy in copies:
        copy.start()
    near = place_ref[0] // sides
    total = sides * slots
    columns = own_ref.shape[-1]
    squares = jnp.zeros((total, 1), f32)
    for k in range(sides):
        block = lax.rem(near + sides - k, sides)
        x = x_ref[:, block].reshape(total, depth).astype(f32)
        squares = squares + jnp.sum(x * x, axis=1, keepdims=True)
        scaled_ref[:, k * depth : (k + 1) * depth] = (x * gain_ref[block]).astype(bf16)
    for copy in copies:
        copy.wait()
    scaled = scaled_ref[...]
    sums = [jnp.dot(scaled, weight_ref[m], preferred_element_type=f32) for m in range(2)]
    second = lax.broadcasted_iota(jnp.int32, (total, 1), 0) % (2 * capacity) >= capacity
    partial = jnp.where(second, sums[1], sums[0])
    high = squares.astype(bf16).astype(f32)
    lane = lax.broadcasted_iota(jnp.int32, (total, 128), 1)
    pieces = jnp.where(lane < 64, high, squares - high)
    size = 2 * capacity
    for a in range(sides):
        for b in range(sides):
            cut = slice((a * sides + b) * size, (a * sides + b + 1) * size)
            state = state_ref[a, b].astype(f32)
            slot_rows = jnp.concatenate([partial[cut], pieces[cut]], axis=1)
            state = jnp.concatenate([state, jnp.zeros_like(state)], axis=1)
            out_ref[b, a] = jnp.concatenate([slot_rows, state], axis=0).astype(bf16)


def activate(got_ref, extra_ref, out_ref, state_ref, *, features):
    blocks, lines, size, _ = got_ref.shape
    extra_rows = 8
    slots = lines * (size - extra_rows)
    width = state_ref.shape[1] // (blocks * lines)
    for a in range(lines):
        for x in range(blocks):
            start = (a * blocks + x) * width
            state = got_ref[x, a, :, :width].astype(f32)[size - extra_rows :]
            state_ref[:, start : start + width] = state

    def total(k):
        value = got_ref[0, :, :, k * 128 : (k + 1) * 128].astype(f32)
        for j in range(1, blocks):
            value = value + got_ref[j, :, :, k * 128 : (k + 1) * 128].astype(f32)
        return value[:, : size - extra_rows].reshape(slots, 128)

    pieces = total(3)
    squares = pieces[:, 0:1] + pieces[:, 64:65]
    norm = lax.rsqrt(squares / features + 1e-6)
    values = []
    for k in range(3):
        both = total(k) * norm
        values.append(both / (1.0 + jnp.exp(-both)) * pltpu.roll(both, 64, 1))
    part = slots // 2
    left = lax.broadcasted_iota(jnp.int32, (slots, 128), 1) < 64
    full = jnp.where(left, values[0], pltpu.roll(values[1], 64, 1)).astype(bf16)
    rest = jnp.where(left[:part], values[2][:part], pltpu.roll(values[2][part:], 64, 1)).astype(bf16)
    extra = extra_ref[...]
    for k in range(out_ref.shape[0]):
        out_ref[k, 0:slots, :] = full
        out_ref[k, slots : slots + part, :] = rest
        out_ref[k, slots + part :, :] = extra


def combine(
    place_ref,
    got_ref,
    own_ref,
    prev_ref,
    next_ref,
    opp_ref,
    opp2_ref,
    out_ref,
    x_ref,
    w_ref,
    *,
    capacity,
):
    w_refs = (
        (own_ref.at[0], own_ref.at[1]),
        (prev_ref.at[0], prev_ref.at[1]),
        (opp_ref, opp2_ref),
        (next_ref.at[0], next_ref.at[1]),
    )
    sides = got_ref.shape[0]
    far = place_ref[0] % sides
    slots = x_ref.shape[0]
    rest = slots // 2
    width = w_ref.shape[2]
    size = got_ref.shape[2] * sides
    left = lax.broadcasted_iota(jnp.int32, (rest, 128), 1) < 64
    for y in range(sides):
        x_ref[:, y * 128 : (y + 1) * 128] = got_ref[y, :slots]
    for y in range(0, sides, 2):
        a, b = (got_ref[k, slots : slots + rest].astype(f32) for k in (y, y + 1))
        cut = slice((sides + y // 2) * 128, (sides + y // 2 + 1) * 128)
        x_ref[:rest, cut] = jnp.where(left, a, pltpu.roll(b, 64, 1)).astype(bf16)
        x_ref[rest:, cut] = jnp.where(left, pltpu.roll(a, 64, 1), b).astype(bf16)
    x = x_ref[...]

    table = got_ref[0, slots + rest :].astype(f32)
    for y in range(1, sides):
        table = table + got_ref[y, slots + rest :].astype(f32)
    table = jnp.concatenate([table[k * 8 : (k + 1) * 8] for k in range(sides)], axis=1)
    code = table.astype(jnp.int32)
    slot = lax.broadcasted_iota(jnp.int32, (slots, size), 0) + 1
    hit_a = slot == code[0:1, :]
    hit_b = slot == code[1:2, :]
    weight_a = table[2:3, :] + table[3:4, :] + table[4:5, :]
    weight_b = table[5:6, :] + table[6:7, :] + table[7:8, :]
    weight = jnp.where(hit_a, weight_a, 0.0) + jnp.where(hit_b, weight_b, 0.0)
    weight = jnp.sum(weight, axis=1, keepdims=True)
    select = (hit_a | hit_b).astype(f32).T.astype(bf16)

    second = lax.broadcasted_iota(jnp.int32, (slots, 1), 0) % (2 * capacity) >= capacity
    for k in range(sides):
        block = lax.rem(far + sides - k, sides)
        for m in range(2):
            for y in range(sides):
                w_ref[m, y * 128 : (y + 1) * 128] = w_refs[k][m][y * 192 : y * 192 + 128]
                start = sides * 128 + y * 64
                w_ref[m, start : start + 64] = w_refs[k][m][y * 192 + 128 : (y + 1) * 192]
        result = jnp.where(
            second,
            jnp.dot(x, w_ref[1], preferred_element_type=f32),
            jnp.dot(x, w_ref[0], preferred_element_type=f32),
        )
        found = jnp.dot(select, (result * weight).astype(bf16), preferred_element_type=f32)
        start = pl.multiple_of(block * width, width)
        out_ref[:, :, :, pl.ds(start, width)] = found.astype(bf16).reshape(sides, -1, 16, width)


def local(
    queries,
    cache,
    new_key_value,
    out_proj,
    residual,
    norm_gain,
    expert_ids,
    gates,
    w_gate_up,
    w_down,
):
    n_seq, n_exp = lax.axis_size("seq"), lax.axis_size("exp")
    n_chip = n_exp // 2
    seq_index, exp_index = lax.axis_index("seq"), lax.axis_index("exp")
    core, chip = exp_index % 2, exp_index // 2
    place = jnp.stack([seq_index, core, chip]).astype(jnp.int32)
    rows, heads, width = queries.shape
    top_k = expert_ids.shape[1]
    features = norm_gain.shape[0]
    members, feature_block, gate_columns = w_gate_up.shape
    hidden_units = w_down.shape[1]
    capacity = 5 * rows * top_k // (4 * members * n_exp)
    swap = [(i, i ^ 1) for i in range(n_exp)]
    near = [[4 * p + i for i in range(4)] for p in range(n_chip // 2)]
    far = [[4 * p + i for p in range(n_chip // 2)] for i in range(4)]
    chips = [[2 * z + c for z in range(n_chip)] for c in range(2)]
    sides = math.isqrt(n_seq)
    along_x = [[sides * y + x for x in range(sides)] for y in range(sides)]
    along_y = [[sides * y + x for y in range(sides)] for x in range(sides)]

    def spots():
        return np.ndindex(sides, sides, sides, sides, 2)

    def flat(y, x, a, b, c):
        return (sides * y + x) * n_exp + 2 * (sides * a + b) + c

    swap_x = [(flat(y, b, a, x, c), flat(y, x, a, b, c)) for y, x, a, b, c in spots()]

    def over_chips(value):
        return lax.all_to_all(value, "exp", 0, 0, tiled=True, axis_index_groups=chips)

    def over_seq(value, groups):
        return lax.all_to_all(value, "seq", 0, 0, tiled=True, axis_index_groups=groups)

    def sum_near(value):
        value = lax.all_to_all(value, "exp", 0, 0, tiled=True, axis_index_groups=near)
        return jnp.sum(value.astype(f32), axis=0).astype(bf16)

    def over_far(value):
        return lax.all_to_all(value, "exp", 0, 0, tiled=True, axis_index_groups=far)

    shift_y, shift_x = {}, {}
    for k in (1, -1):
        shift_y[k] = [
            (sides * y + x, sides * ((y + k) % sides) + x) for y in range(sides) for x in range(sides)
        ]
        shift_x[k] = [
            (sides * y + x, sides * y + (x + k) % sides) for y in range(sides) for x in range(sides)
        ]

    with jax.named_scope("turn_residual"):
        packed = jnp.concatenate([residual, expert_ids.T.astype(bf16)], axis=0)
        turned = lax.ppermute(packed, ("seq", "exp"), swap_x)

    with jax.named_scope("key_values"):
        group = exp_index * heads // (QUERY_HEADS // KEY_VALUE_HEADS)
        own_cache = lax.dynamic_index_in_dim(cache, group, 1, keepdims=False)
        own_fresh = lax.dynamic_index_in_dim(new_key_value, group, 1, keepdims=False)
        own_kv = jnp.concatenate([own_cache, own_fresh], axis=0).transpose(1, 0, 2)
        kv = over_seq(jnp.broadcast_to(own_kv[None], (sides,) + own_kv.shape), along_y)
        q = lax.all_gather(
            queries.transpose(1, 0, 2), "seq", axis=0, tiled=True, axis_index_groups=along_x
        )

    with jax.named_scope("attention"):
        cached = cache.shape[0]
        span = cached + rows
        attended = run(
            functools.partial(attend, rows=rows, cached=cached, scale=1.0 / math.sqrt(width)),
            shape((sides, (sides * heads) * rows + 4 * sides * heads, width)),
            q,
            kv,
            place=place,
            flops=4 * q.size * span * sides,
            moved=kv.size * 2,
            scratch=[pltpu.VMEM((2, heads * rows, sides * span), f32)],
            name="attend",
        )
        columns = lax.all_gather(
            lax.optimization_barrier((out_proj, kv))[0],
            "seq",
            axis=0,
            tiled=True,
            axis_index_groups=along_y,
        )

    with jax.named_scope("projection"):
        part = shape((n_chip, rows, feature_block // 2))
        keep, send = run(
            functools.partial(project, rows=rows),
            [part, part],
            over_seq(attended, along_x),
            columns,
            place=place,
            name="project",
        )
        weights, w_out, send = lax.optimization_barrier((w_gate_up, w_down, send))
        paired = (keep.astype(f32) + lax.ppermute(send, "exp", swap).astype(f32)).astype(bf16)
        piece = (members, feature_block, gate_columns // sides)
        longer = (members + 1,) + piece[1:]
        w_own, w_next, w_prev = run(
            split_columns,
            [shape(piece), shape(longer), shape(longer)],
            weights,
            place=place,
            left=(0,),
            scratch=[
                pltpu.VMEM((sides,) + piece, bf16),
                pltpu.VMEM(w_gate_up.shape, bf16),
                pltpu.SemaphoreType.DMA(()),
            ],
            name="split_columns",
        )
        near_y = (lax.ppermute(w_next, "seq", shift_y[1]), lax.ppermute(w_prev, "seq", shift_y[-1]))
        near_x = (lax.ppermute(w_out, "seq", shift_x[1]), lax.ppermute(w_out, "seq", shift_x[-1]))
        gathered, near_y, near_x = lax.optimization_barrier((over_chips(paired), near_y, near_x))
        own_state = run(
            add_state,
            shape(turned.shape),
            gathered,
            turned,
            name="add_state",
        )
        other_state = lax.ppermute(own_state, "exp", swap)

    with jax.named_scope("gate_up"):
        slots = 2 * capacity
        size = slots + 8
        outgoing = run(
            functools.partial(dispatch, capacity=capacity),
            shape((n_chip, size, feature_block)),
            own_state,
            other_state,
            place=place,
            name="dispatch",
        )
        incoming = over_chips(outgoing)
        far_y = (
            lax.ppermute(near_y[0][members], "seq", shift_y[1]),
            lax.ppermute(near_y[1][members], "seq", shift_y[-1]),
        )
        far_x = (
            lax.ppermute(near_x[0][0], "seq", shift_x[1]),
            lax.ppermute(near_x[1][1], "seq", shift_x[-1]),
        )
        incoming, far_x, far_y = lax.optimization_barrier((incoming, far_x, far_y))
        incoming = incoming.reshape(sides, sides, size, feature_block)
        state = incoming[:, :, slots:]
        incoming = incoming[:, :, :slots].reshape(1, sides, sides * slots, feature_block)
        incoming = over_seq(jnp.broadcast_to(incoming, (sides,) + incoming.shape[1:]), along_y)
        gain = lax.dynamic_index_in_dim(
            norm_gain.reshape(sides, sides, 1, feature_block), seq_index % sides, 1, False
        )
        width = piece[-1] + 128
        partial = run(
            functools.partial(gate_up, capacity=capacity),
            shape((sides, sides, size, width)),
            incoming,
            state,
            gain,
            w_own,
            *near_y,
            *far_y,
            place=place,
            left=range(3, 8),
            room=56,
            scratch=[
                pltpu.VMEM((n_seq * slots, sides * feature_block), bf16),
                pltpu.VMEM((members, sides * feature_block, piece[-1]), bf16),
                pltpu.SemaphoreType.DMA((5,)),
            ],
            name="gate_up",
        )
    with jax.named_scope("tables"):
        expert_ids, gates, partial = lax.optimization_barrier((expert_ids, gates, partial))
        lines = []
        weights = []
        for member in range(2):
            chosen = expert_ids == exp_index * 2 + member
            taken = jnp.sum(chosen.astype(jnp.int32), axis=1)
            slot = jnp.cumsum(taken) - taken
            code = slot + member * capacity + (seq_index // sides) * 2 * capacity + 1
            lines.append(jnp.where(taken > 0, code, 0).astype(f32))
            weight = jnp.sum(jnp.where(chosen, gates, 0.0), axis=1)
            first = lax.reduce_precision(weight, 8, 7)
            second = lax.reduce_precision(weight - first, 8, 7)
            weights += [first, second, weight - first - second]
        table = jnp.stack(lines + weights).reshape(8, n_chip // 2, 2, 2, 1, 4)
        spot = (jnp.arange(sides) == seq_index // sides).astype(f32).reshape(1, 1, 1, 1, sides, 1)
        table = (table * spot).transpose(2, 3, 0, 1, 4, 5)
        extra = table.reshape(4 * 8, rows).astype(bf16)

    with jax.named_scope("down"):
        quarter = sides * slots
        sums = over_seq(partial, along_x)
        active, state = run(
            functools.partial(activate, features=features),
            [shape((sides, quarter + quarter // 2 + extra.shape[0], 128)), shape((8, features), f32)],
            sums,
            extra,
            name="activate",
        )
        line = 4 * sides
        partial = run(
            functools.partial(combine, capacity=capacity),
            shape((4, n_chip // 2, line, sides * feature_block)),
            over_seq(active, along_y),
            w_down,
            *near_x,
            *far_x,
            place=place,
            scratch=[
                pltpu.VMEM((quarter, hidden_units), bf16),
                pltpu.VMEM((members, hidden_units, feature_block), bf16),
            ],
            name="combine",
        )

    with jax.named_scope("output"):
        gathered = over_far(sum_near(partial))
        mixed = jnp.sum(gathered.astype(f32), axis=0).astype(bf16)
        mixed = over_seq(mixed.reshape(sides, 4, sides * feature_block), along_y)
        mixed = mixed.transpose(1, 0, 2).reshape(4, features)
        return (state[:4] + mixed.astype(f32)).astype(bf16)


def solution(mesh):
    in_specs = (
        P("seq", "exp", None),
        P("seq", None, None, None),
        P("seq", None, None, None),
        P("exp", "seq"),
        P("seq", "exp"),
        P(),
        P("seq", None),
        P("seq", None),
        P("exp", "seq", None),
        P("exp", None, "seq"),
    )
    out_specs = P(("seq", "exp"), None)
    return jax.shard_map(local, mesh=mesh, in_specs=in_specs, out_specs=out_specs, check_vma=False)
```

```python
import functools
import math

import jax
import jax.numpy as jnp
import numpy as np
from jax import lax
from jax.experimental import pallas as pl
from jax.experimental.pallas import tpu as pltpu
from jax.sharding import PartitionSpec as P

QUERY_HEADS = 64
KEY_VALUE_HEADS = 4
FLOOR = -1e30
f32 = jnp.float32
bf16 = jnp.bfloat16


def run(body, out_shape, *operands, place=None, left=(), room=16, flops=0, moved=0, scratch=(), name=None):
    vmem = pl.BlockSpec(memory_space=pltpu.VMEM)
    spaces = [
        pl.BlockSpec(memory_space=pl.ANY) if i in left else vmem for i in range(len(operands))
    ]
    smem = pl.BlockSpec(memory_space=pltpu.SMEM)
    placed = [] if place is None else [place]
    return pl.pallas_call(
        body,
        out_shape=out_shape,
        in_specs=[smem] * len(placed) + spaces,
        out_specs=jax.tree.map(lambda _: vmem, out_shape),
        scratch_shapes=list(scratch),
        compiler_params=pltpu.CompilerParams(vmem_limit_bytes=room * 1024 * 1024),
        cost_estimate=pl.CostEstimate(flops=flops, bytes_accessed=moved, transcendentals=0),
        name=name,
    )(*placed, *operands)


def shape(dims, dtype=bf16):
    return jax.ShapeDtypeStruct(dims, dtype)


def attend(place_ref, q_ref, kv_ref, out_ref, s_ref, *, rows, cached, scale):
    sides, _, span, width = kv_ref.shape
    blocks = q_ref.shape[0]
    seq_index = place_ref[0]
    near, far = seq_index // sides, seq_index % sides
    heads = blocks // sides
    total = heads * rows
    lane = lax.broadcasted_iota(jnp.int32, (1, rows), 1)
    pos = [(part * sides + far) * rows + lane for part in range(sides)]
    token = lax.broadcasted_iota(jnp.int32, (total, 1), 0) % rows
    column = lax.broadcasted_iota(jnp.int32, (rows, 128), 1)
    factor = scale * math.log2(math.e)
    logs = jnp.zeros((rows, 128), f32)
    for b in range(sides):
        q = q_ref[b * heads : (b + 1) * heads].reshape(total, width)
        query_pos = (near * sides + b) * rows + token
        top = jnp.full((total, 128), FLOOR, f32)
        for part in range(sides):
            s = lax.dot_general(
                q, kv_ref[part, 0], (((1,), (1,)), ((), ())), preferred_element_type=f32
            )
            fresh = jnp.where(pos[part] <= query_pos, s[:, cached:], FLOOR)
            s_ref[b % 2, :, part * span : part * span + cached] = s[:, :cached]
            s_ref[b % 2, :, part * span + cached : (part + 1) * span] = fresh
            for k in range(cached // 128):
                top = jnp.maximum(top, s[:, k * 128 : (k + 1) * 128])
            for k in range(rows // 128):
                top = jnp.maximum(top, fresh[:, k * 128 : (k + 1) * 128])
        top = jnp.max(top, axis=1, keepdims=True)
        acc = jnp.zeros((total, width), f32)
        sums = jnp.zeros((total, 128), f32)
        for part in range(sides):
            cut = slice(part * span, (part + 1) * span)
            p = jnp.exp2((s_ref[b % 2, :, cut] - top) * factor)
            for k in range(span // 128):
                sums = sums + p[:, k * 128 : (k + 1) * 128]
            acc = acc + jnp.dot(p.astype(bf16), kv_ref[part, 1], preferred_element_type=f32)
        row_sum = jnp.sum(sums, axis=1, keepdims=True)
        part_out = (acc / row_sum).astype(bf16)
        row_log = top * factor + jnp.log2(row_sum)
        for h in range(heads):
            logs = jnp.where(column == b * heads + h, row_log[h * rows : (h + 1) * rows], logs)
        for k in range(out_ref.shape[0]):
            out_ref[k, b * total : (b + 1) * total, :] = part_out
    logs = logs.T[:blocks]
    first = logs.astype(bf16).astype(f32)
    second = (logs - first).astype(bf16).astype(f32)
    third = logs - first - second
    pieces = jnp.concatenate([first, second, third, jnp.zeros_like(first)], axis=0).astype(bf16)
    for k in range(out_ref.shape[0]):
        out_ref[k, blocks * rows :, :] = pieces


def project(place_ref, got_ref, w_ref, keep_ref, send_ref, *, rows):
    sides, _, width = got_ref.shape
    half = place_ref[1]
    depth = w_ref.shape[0] // sides
    heads = depth // width
    blocks = sides * heads
    base = blocks * rows
    logs = []
    for x in range(sides):
        pieces = got_ref[x, base:, :].astype(f32)
        logs.append(pieces[:blocks] + pieces[blocks : 2 * blocks] + pieces[2 * blocks : 3 * blocks])
    top = functools.reduce(jnp.maximum, logs)
    shares = [jnp.exp2(v - top) for v in logs]
    whole = functools.reduce(jnp.add, shares)
    shares = jnp.concatenate([v / whole for v in shares], axis=0).T
    joined = []
    for b in range(sides):
        line = []
        for h in range(heads):
            k = b * heads + h
            value = jnp.zeros((rows, width), f32)
            for x in range(sides):
                share = shares[:, x * blocks + k : x * blocks + k + 1]
                value = value + share * got_ref[x, k * rows : (k + 1) * rows, :].astype(f32)
            line.append(value.astype(bf16))
        joined.append(jnp.concatenate(line, axis=1))
    x = jnp.concatenate(joined, axis=0)
    for a in range(sides):
        y = jnp.dot(x, w_ref[a * depth : (a + 1) * depth, :], preferred_element_type=f32)
        part = y.shape[1] // 2
        low, high = y[:, :part], y[:, part:]
        keep = jnp.where(half == 0, low, high).astype(bf16)
        send = jnp.where(half == 0, high, low).astype(bf16)
        keep_ref[a * sides : (a + 1) * sides] = keep.reshape(sides, rows, part)
        send_ref[a * sides : (a + 1) * sides] = send.reshape(sides, rows, part)


def add_state(got_ref, packed_ref, out_ref):
    rows = got_ref.shape[1]
    total = packed_ref[0:rows, :].astype(f32)
    for k in range(got_ref.shape[0]):
        total = total + got_ref[k].astype(f32)
    out_ref[0:rows, :] = total.astype(bf16)
    out_ref[rows:, :] = packed_ref[rows:, :]


def dispatch(place_ref, own_ref, other_ref, out_ref, *, capacity):
    half = place_ref[1]
    tokens = own_ref.shape[1]
    own, other = own_ref[0:tokens, :], other_ref[0:tokens, :]
    low = jnp.where(half == 0, own.astype(f32), other.astype(f32)).astype(bf16)
    high = jnp.where(half == 0, other.astype(f32), own.astype(f32)).astype(bf16)
    state = jnp.concatenate([low, high], axis=1)
    chips, size, _ = out_ref.shape
    ids = own_ref[tokens:, :].astype(f32).astype(jnp.int32)
    before = (
        lax.broadcasted_iota(jnp.int32, (tokens, tokens), 0)
        < lax.broadcasted_iota(jnp.int32, (tokens, tokens), 1)
    ).astype(f32).astype(bf16)
    codes = []
    for member in range(2):
        expert = lax.broadcasted_iota(jnp.int32, (chips, tokens), 0) * 4 + 2 * half + member
        taken = jnp.zeros((chips, tokens), f32)
        for k in range(ids.shape[0]):
            taken = taken + (expert == ids[k : k + 1, :]).astype(f32)
        slot = jnp.dot(taken.astype(bf16), before, preferred_element_type=f32)
        codes.append(jnp.where(taken > 0, slot.astype(jnp.int32) + member * capacity, -1))
    slots = lax.broadcasted_iota(jnp.int32, (chips, size, tokens), 1)
    chosen = (codes[0][:, None, :] == slots) | (codes[1][:, None, :] == slots)
    place = lax.broadcasted_iota(jnp.int32, (chips, size, tokens), 0) * 8 + 4 * half
    own = slots - 2 * capacity
    token = lax.broadcasted_iota(jnp.int32, (chips, size, tokens), 2)
    chosen = chosen | ((own >= 0) & (own < 4) & (token == place + own))
    select = chosen.astype(f32).reshape(chips * size, tokens).astype(bf16)
    rows = jnp.dot(select, state, preferred_element_type=f32)
    out_ref[...] = rows.astype(bf16).reshape(out_ref.shape)


def split_columns(place_ref, w_in_ref, own_ref, next_ref, prev_ref, all_ref, w_ref, sem):
    copy = pltpu.make_async_copy(w_in_ref, w_ref, sem)
    copy.start()
    copy.wait()
    sides = all_ref.shape[0]
    near = place_ref[0] // sides
    members, depth, columns = w_ref.shape
    left = lax.broadcasted_iota(jnp.int32, (depth, 128), 1) < 64
    for m in range(members):
        for q in range(columns // 128):
            cut = slice(q // 2 * 128, (q // 2 + 1) * 128)
            gate = w_ref[m, :, cut].astype(f32)
            up = w_ref[m, :, columns // 2 + cut.start : columns // 2 + cut.stop].astype(f32)
            if q % 2:
                gate = pltpu.roll(gate, 64, 1)
            else:
                up = pltpu.roll(up, 64, 1)
            per = columns // 128 // sides
            out = slice(q % per * 128, (q % per + 1) * 128)
            all_ref[q // per, m, :, out] = jnp.where(left, gate, up).astype(bf16)
    far = lax.rem(near + 2, sides)
    own_ref[...] = all_ref[near]
    for ref, step, m in ((next_ref, 1, 0), (prev_ref, sides - 1, 1)):
        ref[0:2] = all_ref[lax.rem(near + step, sides)]
        ref[2] = all_ref[far, m]


def gate_up(place_ref, x_ref, state_ref, gain_ref, own_ref, prev_ref, next_ref, opp_ref, opp2_ref, out_ref, scaled_ref, weight_ref, sems, *, capacity):
    sides, _, slots, depth = x_ref.shape
    parts = (
        (own_ref, weight_ref.at[:, 0:depth]),
        (prev_ref.at[0:2], weight_ref.at[:, depth : 2 * depth]),
        (opp_ref, weight_ref.at[0, 2 * depth : 3 * depth]),
        (opp2_ref, weight_ref.at[1, 2 * depth : 3 * depth]),
        (next_ref.at[0:2], weight_ref.at[:, 3 * depth : 4 * depth]),
    )
    copies = [pltpu.make_async_copy(a, b, sems.at[k]) for k, (a, b) in enumerate(parts)]
    for copy in copies:
        copy.start()
    near = place_ref[0] // sides
    total = sides * slots
    columns = own_ref.shape[-1]
    squares = jnp.zeros((total, 1), f32)
    for k in range(sides):
        block = lax.rem(near + sides - k, sides)
        x = x_ref[:, block].reshape(total, depth).astype(f32)
        squares = squares + jnp.sum(x * x, axis=1, keepdims=True)
        scaled_ref[:, k * depth : (k + 1) * depth] = (x * gain_ref[block]).astype(bf16)
    for copy in copies:
        copy.wait()
    scaled = scaled_ref[...]
    sums = [jnp.dot(scaled, weight_ref[m], preferred_element_type=f32) for m in range(2)]
    second = lax.broadcasted_iota(jnp.int32, (total, 1), 0) % (2 * capacity) >= capacity
    partial = jnp.where(second, sums[1], sums[0])
    high = squares.astype(bf16).astype(f32)
    lane = lax.broadcasted_iota(jnp.int32, (total, 128), 1)
    pieces = jnp.where(lane < 64, high, squares - high)
    size = 2 * capacity
    for a in range(sides):
        for b in range(sides):
            cut = slice((a * sides + b) * size, (a * sides + b + 1) * size)
            state = state_ref[a, b].astype(f32)
            slot_rows = jnp.concatenate([partial[cut], pieces[cut]], axis=1)
            state = jnp.concatenate([state, jnp.zeros_like(state)], axis=1)
            out_ref[b, a] = jnp.concatenate([slot_rows, state], axis=0).astype(bf16)


def activate(got_ref, extra_ref, out_ref, state_ref, *, features):
    blocks, lines, size, _ = got_ref.shape
    extra_rows = 8
    slots = lines * (size - extra_rows)
    width = state_ref.shape[1] // (blocks * lines)
    for a in range(lines):
        for x in range(blocks):
            start = (a * blocks + x) * width
            state = got_ref[x, a, :, :width].astype(f32)[size - extra_rows :]
            state_ref[:, start : start + width] = state

    def total(k):
        value = got_ref[0, :, :, k * 128 : (k + 1) * 128].astype(f32)
        for j in range(1, blocks):
            value = value + got_ref[j, :, :, k * 128 : (k + 1) * 128].astype(f32)
        return value[:, : size - extra_rows].reshape(slots, 128)

    pieces = total(3)
    squares = pieces[:, 0:1] + pieces[:, 64:65]
    norm = lax.rsqrt(squares / features + 1e-6)
    values = []
    for k in range(3):
        both = total(k) * norm
        values.append(both / (1.0 + jnp.exp(-both)) * pltpu.roll(both, 64, 1))
    part = slots // 2
    left = lax.broadcasted_iota(jnp.int32, (slots, 128), 1) < 64
    full = jnp.where(left, values[0], pltpu.roll(values[1], 64, 1)).astype(bf16)
    rest = jnp.where(left[:part], values[2][:part], pltpu.roll(values[2][part:], 64, 1)).astype(bf16)
    extra = extra_ref[...]
    for k in range(out_ref.shape[0]):
        out_ref[k, 0:slots, :] = full
        out_ref[k, slots : slots + part, :] = rest
        out_ref[k, slots + part :, :] = extra


def combine(
    place_ref,
    got_ref,
    own_ref,
    prev_ref,
    next_ref,
    opp_ref,
    opp2_ref,
    keep_ref,
    send_ref,
    x_ref,
    w_ref,
    *,
    capacity,
):
    w_refs = (
        (own_ref.at[0], own_ref.at[1]),
        (prev_ref.at[0], prev_ref.at[1]),
        (opp_ref, opp2_ref),
        (next_ref.at[0], next_ref.at[1]),
    )
    sides = got_ref.shape[0]
    far = place_ref[0] % sides
    slots = x_ref.shape[0]
    rest = slots // 2
    width = w_ref.shape[2]
    size = got_ref.shape[2] * sides
    left = lax.broadcasted_iota(jnp.int32, (rest, 128), 1) < 64
    for y in range(sides):
        x_ref[:, y * 128 : (y + 1) * 128] = got_ref[y, :slots]
    for y in range(0, sides, 2):
        a, b = (got_ref[k, slots : slots + rest].astype(f32) for k in (y, y + 1))
        cut = slice((sides + y // 2) * 128, (sides + y // 2 + 1) * 128)
        x_ref[:rest, cut] = jnp.where(left, a, pltpu.roll(b, 64, 1)).astype(bf16)
        x_ref[rest:, cut] = jnp.where(left, pltpu.roll(a, 64, 1), b).astype(bf16)
    x = x_ref[...]

    table = got_ref[0, slots + rest :].astype(f32)
    for y in range(1, sides):
        table = table + got_ref[y, slots + rest :].astype(f32)
    table = jnp.concatenate([table[k * 8 : (k + 1) * 8] for k in range(sides)], axis=1)
    code = table.astype(jnp.int32)
    slot = lax.broadcasted_iota(jnp.int32, (slots, size), 0) + 1
    hit_a = slot == code[0:1, :]
    hit_b = slot == code[1:2, :]
    weight_a = table[2:3, :] + table[3:4, :] + table[4:5, :]
    weight_b = table[5:6, :] + table[6:7, :] + table[7:8, :]
    weight = jnp.where(hit_a, weight_a, 0.0) + jnp.where(hit_b, weight_b, 0.0)
    weight = jnp.sum(weight, axis=1, keepdims=True)
    select = (hit_a | hit_b).astype(f32).T.astype(bf16)

    second = lax.broadcasted_iota(jnp.int32, (slots, 1), 0) % (2 * capacity) >= capacity
    for k in range(sides):
        block = lax.rem(far + sides - k, sides)
        for m in range(2):
            for y in range(sides):
                w_ref[m, y * 128 : (y + 1) * 128] = w_refs[k][m][y * 192 : y * 192 + 128]
                start = sides * 128 + y * 64
                w_ref[m, start : start + 64] = w_refs[k][m][y * 192 + 128 : (y + 1) * 192]
        result = jnp.where(
            second,
            jnp.dot(x, w_ref[1], preferred_element_type=f32),
            jnp.dot(x, w_ref[0], preferred_element_type=f32),
        )
        found = jnp.dot(select, (result * weight).astype(bf16), preferred_element_type=f32)
        start = pl.multiple_of(block * width, width)
        found = found.reshape(sides, -1, 16, width)
        for p in range(2):
            low, high = found[2 * p], found[2 * p + 1]
            keep = jnp.where(place_ref[1] == 0, low, high).astype(bf16)
            send = jnp.where(place_ref[1] == 0, high, low).astype(bf16)
            keep_ref[:, p, :, pl.ds(start, width)] = keep
            send_ref[:, p, :, pl.ds(start, width)] = send


def local(
    queries,
    cache,
    new_key_value,
    out_proj,
    residual,
    norm_gain,
    expert_ids,
    gates,
    w_gate_up,
    w_down,
):
    n_seq, n_exp = lax.axis_size("seq"), lax.axis_size("exp")
    n_chip = n_exp // 2
    seq_index, exp_index = lax.axis_index("seq"), lax.axis_index("exp")
    core, chip = exp_index % 2, exp_index // 2
    place = jnp.stack([seq_index, core, chip]).astype(jnp.int32)
    rows, heads, width = queries.shape
    top_k = expert_ids.shape[1]
    features = norm_gain.shape[0]
    members, feature_block, gate_columns = w_gate_up.shape
    hidden_units = w_down.shape[1]
    capacity = 5 * rows * top_k // (4 * members * n_exp)
    swap = [(i, i ^ 1) for i in range(n_exp)]
    near = [[4 * p + i for i in range(4)] for p in range(n_chip // 2)]
    far = [[4 * p + i for p in range(n_chip // 2)] for i in range(4)]
    chips = [[2 * z + c for z in range(n_chip)] for c in range(2)]
    sides = math.isqrt(n_seq)
    along_x = [[sides * y + x for x in range(sides)] for y in range(sides)]
    along_y = [[sides * y + x for y in range(sides)] for x in range(sides)]

    def spots():
        return np.ndindex(sides, sides, sides, sides, 2)

    def flat(y, x, a, b, c):
        return (sides * y + x) * n_exp + 2 * (sides * a + b) + c

    swap_x = [(flat(y, b, a, x, c), flat(y, x, a, b, c)) for y, x, a, b, c in spots()]

    def over_chips(value):
        return lax.all_to_all(value, "exp", 0, 0, tiled=True, axis_index_groups=chips)

    def over_seq(value, groups):
        return lax.all_to_all(value, "seq", 0, 0, tiled=True, axis_index_groups=groups)

    def sum_near(value):
        value = lax.all_to_all(value, "exp", 0, 0, tiled=True, axis_index_groups=near)
        return jnp.sum(value.astype(f32), axis=0).astype(bf16)

    def over_far(value):
        return lax.all_to_all(value, "exp", 0, 0, tiled=True, axis_index_groups=far)

    shift_y, shift_x = {}, {}
    for k in (1, -1):
        shift_y[k] = [
            (sides * y + x, sides * ((y + k) % sides) + x) for y in range(sides) for x in range(sides)
        ]
        shift_x[k] = [
            (sides * y + x, sides * y + (x + k) % sides) for y in range(sides) for x in range(sides)
        ]

    with jax.named_scope("turn_residual"):
        packed = jnp.concatenate([residual, expert_ids.T.astype(bf16)], axis=0)
        turned = lax.ppermute(packed, ("seq", "exp"), swap_x)

    with jax.named_scope("key_values"):
        group = exp_index * heads // (QUERY_HEADS // KEY_VALUE_HEADS)
        own_cache = lax.dynamic_index_in_dim(cache, group, 1, keepdims=False)
        own_fresh = lax.dynamic_index_in_dim(new_key_value, group, 1, keepdims=False)
        own_kv = jnp.concatenate([own_cache, own_fresh], axis=0).transpose(1, 0, 2)
        kv = over_seq(jnp.broadcast_to(own_kv[None], (sides,) + own_kv.shape), along_y)
        q = lax.all_gather(
            queries.transpose(1, 0, 2), "seq", axis=0, tiled=True, axis_index_groups=along_x
        )

    with jax.named_scope("attention"):
        cached = cache.shape[0]
        span = cached + rows
        attended = run(
            functools.partial(attend, rows=rows, cached=cached, scale=1.0 / math.sqrt(width)),
            shape((sides, (sides * heads) * rows + 4 * sides * heads, width)),
            q,
            kv,
            place=place,
            flops=4 * q.size * span * sides,
            moved=kv.size * 2,
            scratch=[pltpu.VMEM((2, heads * rows, sides * span), f32)],
            name="attend",
        )
        columns = lax.all_gather(
            lax.optimization_barrier((out_proj, kv))[0],
            "seq",
            axis=0,
            tiled=True,
            axis_index_groups=along_y,
        )

    with jax.named_scope("projection"):
        part = shape((n_chip, rows, feature_block // 2))
        keep, send = run(
            functools.partial(project, rows=rows),
            [part, part],
            over_seq(attended, along_x),
            columns,
            place=place,
            name="project",
        )
        weights, w_out, send = lax.optimization_barrier((w_gate_up, w_down, send))
        paired = (keep.astype(f32) + lax.ppermute(send, "exp", swap).astype(f32)).astype(bf16)
        piece = (members, feature_block, gate_columns // sides)
        longer = (members + 1,) + piece[1:]
        w_own, w_next, w_prev = run(
            split_columns,
            [shape(piece), shape(longer), shape(longer)],
            weights,
            place=place,
            left=(0,),
            scratch=[
                pltpu.VMEM((sides,) + piece, bf16),
                pltpu.VMEM(w_gate_up.shape, bf16),
                pltpu.SemaphoreType.DMA(()),
            ],
            name="split_columns",
        )
        near_y = (lax.ppermute(w_next, "seq", shift_y[1]), lax.ppermute(w_prev, "seq", shift_y[-1]))
        near_x = (lax.ppermute(w_out, "seq", shift_x[1]), lax.ppermute(w_out, "seq", shift_x[-1]))
        gathered, near_y, near_x = lax.optimization_barrier((over_chips(paired), near_y, near_x))
        own_state = run(
            add_state,
            shape(turned.shape),
            gathered,
            turned,
            name="add_state",
        )
        other_state = lax.ppermute(own_state, "exp", swap)

    with jax.named_scope("gate_up"):
        slots = 2 * capacity
        size = slots + 8
        outgoing = run(
            functools.partial(dispatch, capacity=capacity),
            shape((n_chip, size, feature_block)),
            own_state,
            other_state,
            place=place,
            name="dispatch",
        )
        incoming = over_chips(outgoing)
        far_y = (
            lax.ppermute(near_y[0][members], "seq", shift_y[1]),
            lax.ppermute(near_y[1][members], "seq", shift_y[-1]),
        )
        far_x = (
            lax.ppermute(near_x[0][0], "seq", shift_x[1]),
            lax.ppermute(near_x[1][1], "seq", shift_x[-1]),
        )
        incoming, far_x, far_y = lax.optimization_barrier((incoming, far_x, far_y))
        incoming = incoming.reshape(sides, sides, size, feature_block)
        state = incoming[:, :, slots:]
        incoming = incoming[:, :, :slots].reshape(1, sides, sides * slots, feature_block)
        incoming = over_seq(jnp.broadcast_to(incoming, (sides,) + incoming.shape[1:]), along_y)
        gain = lax.dynamic_index_in_dim(
            norm_gain.reshape(sides, sides, 1, feature_block), seq_index % sides, 1, False
        )
        width = piece[-1] + 128
        partial = run(
            functools.partial(gate_up, capacity=capacity),
            shape((sides, sides, size, width)),
            incoming,
            state,
            gain,
            w_own,
            *near_y,
            *far_y,
            place=place,
            left=range(3, 8),
            room=56,
            scratch=[
                pltpu.VMEM((n_seq * slots, sides * feature_block), bf16),
                pltpu.VMEM((members, sides * feature_block, piece[-1]), bf16),
                pltpu.SemaphoreType.DMA((5,)),
            ],
            name="gate_up",
        )
    with jax.named_scope("tables"):
        expert_ids, gates, partial = lax.optimization_barrier((expert_ids, gates, partial))
        lines = []
        weights = []
        for member in range(2):
            chosen = expert_ids == exp_index * 2 + member
            taken = jnp.sum(chosen.astype(jnp.int32), axis=1)
            slot = jnp.cumsum(taken) - taken
            code = slot + member * capacity + (seq_index // sides) * 2 * capacity + 1
            lines.append(jnp.where(taken > 0, code, 0).astype(f32))
            weight = jnp.sum(jnp.where(chosen, gates, 0.0), axis=1)
            first = lax.reduce_precision(weight, 8, 7)
            second = lax.reduce_precision(weight - first, 8, 7)
            weights += [first, second, weight - first - second]
        table = jnp.stack(lines + weights).reshape(8, n_chip // 2, 2, 2, 1, 4)
        spot = (jnp.arange(sides) == seq_index // sides).astype(f32).reshape(1, 1, 1, 1, sides, 1)
        table = (table * spot).transpose(2, 3, 0, 1, 4, 5)
        extra = table.reshape(4 * 8, rows).astype(bf16)

    with jax.named_scope("down"):
        quarter = sides * slots
        sums = over_seq(partial, along_x)
        active, state = run(
            functools.partial(activate, features=features),
            [shape((sides, quarter + quarter // 2 + extra.shape[0], 128)), shape((8, features), f32)],
            sums,
            extra,
            name="activate",
        )
        line = 4 * sides
        part = shape((n_chip // 2, 2, line, sides * feature_block))
        keep, send = run(
            functools.partial(combine, capacity=capacity),
            [part, part],
            over_seq(active, along_y),
            w_down,
            *near_x,
            *far_x,
            place=place,
            scratch=[
                pltpu.VMEM((quarter, hidden_units), bf16),
                pltpu.VMEM((members, hidden_units, feature_block), bf16),
            ],
            name="combine",
        )

    with jax.named_scope("output"):
        paired = (keep.astype(f32) + lax.ppermute(send, "exp", swap).astype(f32)).astype(bf16)
        gathered = over_chips(paired.reshape(n_chip, line, sides * feature_block))
        mixed = jnp.sum(gathered.astype(f32), axis=0).astype(bf16)
        mixed = over_seq(mixed.reshape(sides, 4, sides * feature_block), along_y)
        mixed = mixed.transpose(1, 0, 2).reshape(4, features)
        return (state[:4] + mixed.astype(f32)).astype(bf16)


def solution(mesh):
    in_specs = (
        P("seq", "exp", None),
        P("seq", None, None, None),
        P("seq", None, None, None),
        P("exp", "seq"),
        P("seq", "exp"),
        P(),
        P("seq", None),
        P("seq", None),
        P("exp", "seq", None),
        P("exp", None, "seq"),
    )
    out_specs = P(("seq", "exp"), None)
    return jax.shard_map(local, mesh=mesh, in_specs=in_specs, out_specs=out_specs, check_vma=False)
```
